128 devices in a mesh: rows: 64 (over z, y, x), sub: 2 (over core).
Axes of the slice: x: 4, y: 4, z: 4, core: 2. Of those that a mesh axis runs over, the one named last changes fastest.
Arguments:
- points: bfloat16 [262144, 1024], P(('rows', 'sub')), may hold values from -192 to 192
- assign: int32 [262144], P(('rows', 'sub')), may hold values from 0 to 65535, as said below
- cluster_counts: int32 [65536], P(('rows', 'sub')), may hold values from 0 to 512, as said below
- centroids: float32 [65536, 1024], P(('rows', 'sub')), may hold values from -6 to 6
- codebook: float32 [8, 256, 128], P('sub'), may hold values from -8 to 8
Outputs:
- rebuilt: bfloat16 [262144, 1024], P(('rows', 'sub'))
- moved_centroids: float32 [65536, 1024], P(('rows', 'sub'))
- moved_codebook: float32 [8, 256, 128], P('sub')
The draws below stay inside these ranges and needn't reach their ends.
Inputs may be any that keep to these rules, and one draw needn't show every extreme that they name: Within each device block (rows b * 2048 to (b + 1) * 2048 - 1) assign does not fall. The rows of device block b name clusters of centroid block b (clusters b * 512 to (b + 1) * 512 - 1), or of the top 64 clusters of block b - 1, or of the bottom 64 clusters of block b + 1; every device block except the first has 1 to 512 rows in the block below, every one except the last has 1 to 512 rows in the block above, and some device block has exactly 512 in the block below and some exactly 512 in the block above. cluster_counts[k] is the number of rows with assign = k; some cluster holds exactly 512 rows.
All inputs are finite; a program needn't handle non-finite values.
Results may differ from the reference program's by a relative error of at most 0.001.
The reference program's roundings to bfloat16 on the way count: a program that leaves them out, or rounds other values in their place, can miss the bound.
Values may be sent and summed in bfloat16 or wider, within the bound.
No kernel may reach another device: no remote copies, remote signals or barrier semaphores. Data moves between devices by JAX's collectives and lax.ppermute only.
A program may use at most 128 MiB of HBM per device.

```python
import math
import jax
import jax.numpy as jnp
from jax import lax

D = 1024
K = 65536
SUBSPACES = 8
CODES = 256
RIM = 64
ROWS_DEV = 2048
ROWS = 262144
K_BLK = 512
SUBDIM = 128
SPILL = 512


def assign_pair(key):
    base_key = jax.random.fold_in(key, 7)
    shards = ROWS // ROWS_DEV
    keys = jax.random.split(base_key, 6)
    spills_up = jax.random.randint(keys[0], (shards - 1,), 1, SPILL + 1)
    spills_down = jax.random.randint(keys[1], (shards - 1,), 1, SPILL + 1)
    picked = jax.random.permutation(keys[2], shards - 1)
    spills_up = spills_up.at[picked[0]].set(SPILL)
    spills_down = spills_down.at[picked[1]].set(SPILL)
    zero_one = jnp.zeros((1,), jnp.int32)
    upward = jnp.concatenate([spills_up, zero_one])
    downward = jnp.concatenate([zero_one, spills_down])
    shard_ids = jnp.arange(shards, dtype=jnp.int32)[:, None]
    slot_ids = jnp.arange(ROWS_DEV, dtype=jnp.int32)[None, :]
    middle_span = K_BLK - 2 * RIM
    below = jnp.sort(jax.random.randint(keys[3], (shards, ROWS_DEV), 0, RIM), axis=1) + (shard_ids - 1) * K_BLK + K_BLK - RIM
    spread_ids = slot_ids * middle_span // ROWS_DEV
    jitter = jax.random.randint(keys[4], (shards, ROWS_DEV), 0, 2)
    middle_local = jnp.sort(jnp.minimum(spread_ids + jitter, middle_span - 1), axis=1)
    middle = middle_local + shard_ids * K_BLK + RIM
    above = jnp.sort(jax.random.randint(keys[5], (shards, ROWS_DEV), 0, RIM), axis=1) + (shard_ids + 1) * K_BLK
    above = jnp.where(shard_ids == picked[0], (shard_ids + 1) * K_BLK + jnp.zeros_like(above), above)
    chosen = jnp.where(slot_ids < downward[:, None], below, jnp.where(slot_ids >= ROWS_DEV - upward[:, None], above, middle))
    return chosen.reshape(-1).astype(jnp.int32)


def draw_assign(key, part):
    return assign_pair(key)


def draw_cluster_counts(key, part):
    chosen = assign_pair(key)
    return jax.ops.segment_sum(jnp.ones_like(chosen), chosen, num_segments=K).astype(jnp.int32)


def draw_points(key, part):
    values = jnp.clip(jax.random.normal(key, (ROWS, D), jnp.float32), -6.0, 6.0)
    return values.astype(jnp.bfloat16)


def levels(own_key, shape, cuts, smallest, top_value):
    loudness = 1.0
    for axis_at, parts in cuts:
        steps = jax.random.uniform(jax.random.fold_in(jax.random.fold_in(own_key, 6), axis_at), (parts,), jnp.float32, smallest / len(cuts), top_value / len(cuts))
        loudness = loudness * jnp.repeat(jnp.exp(steps), shape[axis_at] // parts).reshape((-1,) + (1,) * (len(shape) - 1 - axis_at))
    return loudness


def normal_values(stream_key, dims, deviation, most, cuts=(), held_as=jnp.bfloat16):
    level = levels(stream_key, dims, cuts, -0.22, 0.18) if cuts else 1.0
    entries = jax.random.normal(stream_key, dims, jnp.float32) * deviation * level
    return jnp.minimum(jnp.maximum(entries, -most), most).astype(held_as)


def setup_inputs(seed: int = 0) -> dict:
    arg_keys = jax.random.split(jax.random.key(seed), 6)
    return {
        "points": draw_points(jax.random.fold_in(arg_keys[5], 71), 0),
        "assign": draw_assign(jax.random.fold_in(arg_keys[5], 71), 0),
        "cluster_counts": draw_cluster_counts(jax.random.fold_in(arg_keys[5], 71), 0),
        "centroids": normal_values(arg_keys[3], (K, D), 1.0, 6.0, ((0, 128),), jnp.float32),
        "codebook": normal_values(arg_keys[4], (SUBSPACES, CODES, SUBDIM), 1.4, 8.0, ((0, 2),), jnp.float32),
    }


def reference(points, assign, cluster_counts, centroids, codebook):
    residual = (points.astype(jnp.float32) - jnp.take(centroids, assign, axis=0)).astype(jnp.bfloat16)
    cluster_sums = jax.ops.segment_sum(points.astype(jnp.float32), assign, num_segments=K)
    counts_real = cluster_counts.astype(jnp.float32)
    moved_centroids = (cluster_sums + 2.0 * centroids) / (counts_real + 2.0)[:, None]
    prior_mass = ROWS / CODES
    scale_root = math.sqrt(SUBDIM)

    def one_subspace(which):
        part_rows = lax.dynamic_slice_in_dim(residual, which * SUBDIM, SUBDIM, 1)
        words = lax.dynamic_index_in_dim(codebook, which, 0, keepdims=False)
        words_low = words.astype(jnp.bfloat16)
        dot_terms = jnp.dot(part_rows, words_low.T, preferred_element_type=jnp.float32)
        code_norm = lax.optimization_barrier(jnp.sum(words * words, axis=1))
        logits = (2.0 * dot_terms - code_norm[None, :]) / scale_root
        weights = jax.nn.softmax(logits, axis=-1)
        weights_low = weights.astype(jnp.bfloat16)
        rebuilt_part = jnp.dot(weights_low, words_low, preferred_element_type=jnp.float32).astype(jnp.bfloat16)
        code_sums = jnp.dot(weights_low.T, part_rows, preferred_element_type=jnp.float32)
        code_mass = lax.optimization_barrier(jnp.sum(weights, axis=0))
        moved_words = (code_sums + prior_mass * words) / (code_mass + prior_mass)[:, None]
        return (rebuilt_part, moved_words)
    rebuilt_parts, moved_codebook = lax.map(one_subspace, jnp.arange(SUBSPACES, dtype=jnp.int32))
    rebuilt = jnp.transpose(rebuilt_parts, (1, 0, 2)).reshape(ROWS, D)
    return (rebuilt, moved_centroids, moved_codebook)
```

```python
import math

import jax
import jax.numpy as jnp
from jax import lax
from jax.experimental import pallas as pl
from jax.experimental.pallas import tpu as pltpu
from jax.sharding import PartitionSpec as P

RIM = 64
TILE = 128
STEP = 256
MESH_AXES = ("rows", "sub")
NN = (((1,), (0,)), ((), ()))
NT = (((1,), (1,)), ((), ()))
TN = (((0,), (0,)), ((), ()))


def row_of_ids(ids_ref, first, count, base):
    parts = [ids_ref[pl.ds(first + k, 1), :] for k in range(count)]
    return jnp.concatenate(parts, axis=1) - base


def picks(ids_row, tile):
    slots = lax.broadcasted_iota(jnp.int32, (TILE, ids_row.shape[1]), 0) + tile * TILE
    return (slots == ids_row).astype(jnp.float32).astype(jnp.bfloat16)


def tile_range(ids_smem, base, step):
    first = (ids_smem[step * STEP] - base) // TILE
    last = (ids_smem[step * STEP + STEP - 1] - base) // TILE
    return first, last


def sums_kernel(ids_smem, base_smem, ids_ref, points_ref, counts_ref, cent_ref, moved_ref, down_ref, up_ref, acc):
    step = pl.program_id(0)
    base = base_smem[0]

    @pl.when(step == 0)
    def _():
        acc[...] = jnp.zeros_like(acc)

    first, last = tile_range(ids_smem, base, step)
    ids_row = row_of_ids(ids_ref, step * (STEP // 128), STEP // 128, base)

    def add(tile, carry):
        at = pl.ds(pl.multiple_of(tile * TILE, TILE), TILE)
        acc[at, :] += lax.dot_general(picks(ids_row, tile), points_ref[...], NN, preferred_element_type=jnp.float32)
        return carry

    lax.fori_loop(first, last + 1, add, 0)

    @pl.when(step == pl.num_programs(0) - 1)
    def _():
        own = cent_ref.shape[0]
        down_ref[...] = acc[:RIM].astype(jnp.bfloat16)
        up_ref[...] = acc[RIM + own :].astype(jnp.bfloat16)
        for part in range(own // 128):
            count = jnp.broadcast_to(counts_ref[part : part + 1, :], (128, 128)).astype(jnp.float32)
            inverse = (1.0 / (count + 2.0)).T
            lo = 64 if part == 0 else 0
            hi = 64 if part == own // 128 - 1 else 128
            at = slice(part * 128 + lo, part * 128 + hi)
            for col in range(cent_ref.shape[1] // 128):
                cols = slice(col * 128, col * 128 + 128)
                moved_ref[at, cols] = (
                    acc[RIM + part * 128 + lo : RIM + part * 128 + hi, cols] + 2.0 * cent_ref[at, cols]
                ) * inverse[lo:hi]
        moved_ref[:RIM, :] = acc[RIM : 2 * RIM]
        moved_ref[own - RIM :, :] = acc[own : own + RIM]


def edge_kernel(moved_in, low_in, high_in, counts_ref, cent_ref, moved_ref):
    which = pl.program_id(0)
    row = jnp.where(which == 0, 0, counts_ref.shape[0] - 1)
    count = jnp.broadcast_to(counts_ref[pl.ds(row, 1), :], (128, 128)).astype(jnp.float32)
    inverse = (1.0 / (count + 2.0)).T
    inverse = jnp.where(which == 0, inverse[:RIM], inverse[RIM:])
    spread = jnp.where(which == 0, low_in[...].astype(jnp.float32), high_in[...].astype(jnp.float32))
    for col in range(cent_ref.shape[1] // 128):
        cols = slice(col * 128, col * 128 + 128)
        moved_ref[:, cols] = (moved_in[:, cols] + spread[:, cols] + 2.0 * cent_ref[:, cols]) * inverse


def quant_kernel(
    ids_smem, base_smem, ids_ref, points_ref, cent_ref, low_ref, high_ref, books_ref,
    rebuilt_ref, payload_ref, window3, gathered, resid, books_low, books_t, norms, totals, mass,
):
    step = pl.program_id(0)
    base = base_smem[0]
    subs, codes, subdim = books_ref.shape
    rate = 1.0 / (math.sqrt(subdim) * math.log(2.0))
    own = cent_ref.shape[0]

    @pl.when(step == 0)
    def _():
        def split(value, tile, at):
            hi = value.astype(jnp.bfloat16)
            rest = value - hi.astype(jnp.float32)
            mid = rest.astype(jnp.bfloat16)
            lo = (rest - mid.astype(jnp.float32)).astype(jnp.bfloat16)
            count = value.shape[0]
            for k, piece in enumerate((hi, mid, lo)):
                window3[tile, k * TILE + at : k * TILE + at + count, :] = piece

        split(low_ref[...], 0, 0)
        split(high_ref[...], window3.shape[0] - 1, RIM)
        for part in range(own // RIM):
            tile, at = divmod(part + 1, TILE // RIM)
            split(cent_ref[part * RIM : part * RIM + RIM, :], tile, at * RIM)
        for j in range(subs):
            words = books_ref[j]
            low = words.astype(jnp.bfloat16)
            books_low[j] = low
            books_t[j] = words.T.astype(jnp.bfloat16)
            norm = jnp.sum(words * words, axis=1, keepdims=True) * rate
            norms[j] = jnp.broadcast_to(norm, (codes, 128))
        totals[...] = jnp.zeros_like(totals)
        mass[...] = jnp.zeros_like(mass)

    first, last = tile_range(ids_smem, base, step)
    ids_row = row_of_ids(ids_ref, step * (STEP // 128), STEP // 128, base)

    def fetch(tile):
        pick = picks(ids_row, tile)
        pick3 = jnp.concatenate([pick, pick, pick], axis=0)
        return lax.dot_general(pick3, window3[tile], TN, preferred_element_type=jnp.float32)

    gathered[...] = fetch(first)

    def more(tile, carry):
        gathered[...] += fetch(tile)
        return carry

    lax.fori_loop(first + 1, last + 1, more, 0)
    resid[...] = (points_ref[...].astype(jnp.float32) - gathered[...]).astype(jnp.bfloat16)

    for j in range(subs):
        cols = slice(j * subdim, (j + 1) * subdim)
        rows_j = resid[:, cols]
        dots = lax.dot_general(books_low[j], rows_j, NT, preferred_element_type=jnp.float32)
        weights_low = []
        for part in range(STEP // 128):
            lanes = slice(part * 128, part * 128 + 128)
            logits = dots[:, lanes] * (2.0 * rate) - norms[j]
            top = jnp.max(logits, axis=0, keepdims=True)
            raised = jnp.exp2(logits - top)
            weights = raised * (1.0 / jnp.sum(raised, axis=0, keepdims=True))
            mass[j] += weights
            weights_low.append(weights.astype(jnp.bfloat16))
        weights_low = jnp.concatenate(weights_low, axis=1)
        totals[j] += lax.dot_general(weights_low, rows_j, NN, preferred_element_type=jnp.float32)
        rebuilt_t = lax.dot_general(books_t[j], weights_low, NN, preferred_element_type=jnp.float32)
        rebuilt_ref[:, cols] = rebuilt_t.T.astype(jnp.bfloat16)

    @pl.when(step == pl.num_programs(0) - 1)
    def _():
        half = subs // 2
        group = codes * half // payload_ref.shape[1]
        left = lax.broadcasted_iota(jnp.int32, (8, 128), 1) < 64
        for j in range(subs):
            for g in range(codes // group):
                at = slice(g * group, g * group + group)
                slot = (j % half) * (codes // group) + g
                payload_ref[j // half, slot, :group, :] = totals[j, at, :]
                part = mass[j, at, :]
                part = part + pltpu.roll(part, 64, 1)
                payload_ref[j // half, slot, group:, :] = jnp.where(left, part[:8], part[8:])


def reduce_kernel(prior, parts_ref, book_ref, out_ref):
    total = jnp.sum(parts_ref[...], axis=0)
    group = book_ref.shape[0]
    left = lax.broadcasted_iota(jnp.int32, (8, 128), 1) < 64
    packed = total[group:]
    mass = jnp.concatenate(
        [
            jnp.sum(jnp.where(left, packed, 0.0), axis=1, keepdims=True),
            jnp.sum(jnp.where(left, 0.0, packed), axis=1, keepdims=True),
        ],
        axis=0,
    )
    moved = (total[:group] + prior * book_ref[...]) / (mass + prior)
    out_ref[...] = jnp.broadcast_to(moved[None], out_ref.shape)


def whole(shape):
    return pl.BlockSpec(shape, lambda *_: (0,) * len(shape))


def body(points, assign, cluster_counts, centroids, codebook):
    own, width = centroids.shape
    rows_here = points.shape[0]
    half, codes, subdim = codebook.shape
    rows_axis, sub_axis = MESH_AXES
    owners = lax.axis_size(rows_axis)
    places = owners * lax.axis_size(sub_axis)
    sub = lax.axis_index(sub_axis)
    position = lax.axis_index(rows_axis) * lax.axis_size(sub_axis) + sub
    base = jnp.reshape(position * own - RIM, (1,)).astype(jnp.int32)
    up = [(i, i + 1) for i in range(places - 1)]
    down = [(i + 1, i) for i in range(places - 1)]
    swap = [(0, 1), (1, 0)]
    low = lax.ppermute(centroids[own - RIM :], MESH_AXES, up)
    high = lax.ppermute(centroids[:RIM], MESH_AXES, down)
    other_book = lax.ppermute(codebook, sub_axis, swap)
    ids = assign.reshape(rows_here // 128, 128)
    counts = cluster_counts.reshape(own // 128, 128)
    steps = rows_here // STEP
    slots = own + 2 * RIM
    tile_rows = pl.BlockSpec((STEP, width), lambda i, *_: (i, 0))
    params = pltpu.CompilerParams(vmem_limit_bytes=56 * 1024 * 1024)

    sums, sum_down, sum_up = pl.pallas_call(
        sums_kernel,
        grid_spec=pltpu.PrefetchScalarGridSpec(
            num_scalar_prefetch=2,
            grid=(steps,),
            in_specs=[whole(ids.shape), tile_rows, whole(counts.shape), whole(centroids.shape)],
            out_specs=[whole(centroids.shape), whole((RIM, width)), whole((RIM, width))],
            scratch_shapes=[pltpu.VMEM((slots, width), jnp.float32)],
        ),
        out_shape=[
            jax.ShapeDtypeStruct(centroids.shape, jnp.float32),
            jax.ShapeDtypeStruct((RIM, width), jnp.bfloat16),
            jax.ShapeDtypeStruct((RIM, width), jnp.bfloat16),
        ],
        compiler_params=params,
        cost_estimate=pl.CostEstimate(flops=2 * 10**9, bytes_accessed=8 * 10**6, transcendentals=0),
        name="cluster_sums",
    )(assign, base, ids, points, counts, centroids)

    sum_low = lax.ppermute(sum_up, MESH_AXES, up)
    sum_high = lax.ppermute(sum_down, MESH_AXES, down)

    books = jnp.where(
        sub == 0,
        jnp.concatenate([codebook, other_book], axis=0),
        jnp.concatenate([other_book, codebook], axis=0),
    )
    subs = 2 * half
    group = half * codes // owners
    rebuilt, payload = pl.pallas_call(
        quant_kernel,
        grid_spec=pltpu.PrefetchScalarGridSpec(
            num_scalar_prefetch=2,
            grid=(steps,),
            in_specs=[
                whole(ids.shape), tile_rows, whole(centroids.shape),
                whole((RIM, width)), whole((RIM, width)), whole(books.shape),
            ],
            out_specs=[tile_rows, whole((2, owners, group + 8, subdim))],
            scratch_shapes=[
                pltpu.VMEM((slots // TILE, 3 * TILE, width), jnp.bfloat16),
                pltpu.VMEM((STEP, width), jnp.float32),
                pltpu.VMEM((STEP, width), jnp.bfloat16),
                pltpu.VMEM((subs, codes, subdim), jnp.bfloat16),
                pltpu.VMEM((subs, subdim, codes), jnp.bfloat16),
                pltpu.VMEM((subs, codes, 128), jnp.float32),
                pltpu.VMEM((subs, codes, subdim), jnp.float32),
                pltpu.VMEM((subs, codes, 128), jnp.float32),
            ],
        ),
        out_shape=[
            jax.ShapeDtypeStruct(points.shape, jnp.bfloat16),
            jax.ShapeDtypeStruct((2, owners, group + 8, subdim), jnp.float32),
        ],
        compiler_params=params,
        cost_estimate=pl.CostEstimate(flops=8 * 10**9, bytes_accessed=12 * 10**6, transcendentals=4 * 10**6),
        name="quantize",
    )(assign, base, ids, points, centroids, low, high, books)

    edge = pl.BlockSpec((RIM, width), lambda i: (i * (own // RIM - 1), 0))
    moved_centroids = pl.pallas_call(
        edge_kernel,
        grid=(2,),
        in_specs=[edge, whole((RIM, width)), whole((RIM, width)), whole(counts.shape), edge],
        out_specs=edge,
        out_shape=jax.ShapeDtypeStruct(centroids.shape, jnp.float32),
        input_output_aliases={0: 0},
        name="edge_clusters",
    )(sums, sum_low, sum_high, counts, centroids)

    mine = lax.dynamic_index_in_dim(payload, sub, 0, keepdims=False)
    theirs = lax.dynamic_index_in_dim(payload, 1 - sub, 0, keepdims=False)
    chip = mine + lax.ppermute(theirs, sub_axis, swap)
    parts = lax.all_to_all(chip, rows_axis, 0, 0, tiled=True)
    book_rows = lax.dynamic_slice_in_dim(
        codebook.reshape(half * codes, subdim), lax.axis_index(rows_axis) * group, group, 0
    )
    prior = rows_here * places / codes
    moved = pl.pallas_call(
        lambda *refs: reduce_kernel(prior, *refs),
        out_shape=jax.ShapeDtypeStruct((owners, group, subdim), jnp.float32),
        name="moved_codes",
    )(parts, book_rows)
    moved = lax.all_to_all(moved, rows_axis, 0, 0, tiled=True)
    return (rebuilt, moved_centroids, moved.reshape(codebook.shape))


def solution(mesh):
    both = P(("rows", "sub"), None)
    flat = P(("rows", "sub"))
    books = P("sub", None, None)
    return jax.shard_map(
        body,
        mesh=mesh,
        in_specs=(both, flat, flat, both, books),
        out_specs=(both, both, books),
        check_vma=False,
    )
```

```python
import functools
import math

import jax
import jax.numpy as jnp
from jax import lax
from jax.experimental import pallas as pl
from jax.experimental.pallas import tpu as pltpu
from jax.sharding import PartitionSpec as P

RIM = 64
TILE = 256
CHUNK = 512
COLS = 256
SPAN = 80
PIECES = 3
DEPTH = 256
MESH_AXES = ("rows", "sub")
NT = (((1,), (1,)), ((), ()))
TN = (((0,), (0,)), ((), ()))


def window_starts(ids_smem, base, tile, slots):
    first = ids_smem[tile * TILE] - base
    last = ids_smem[tile * TILE + TILE - 1] - base
    head = jnp.minimum((first // 16) * 16, slots - SPAN)
    tail = jnp.clip((last // 16) * 16 - (SPAN - 16), 0, slots - SPAN)
    return pl.multiple_of(head, 16), pl.multiple_of(tail, 16), last


def note_gaps(ids_smem, ids_ref, base, slots, gaps):
    per = TILE // 128
    missed = jnp.zeros((per, 128), jnp.float32)
    for tile in range(ids_ref.shape[0] // per):
        head, tail, _ = window_starts(ids_smem, base, tile, slots)
        ids = ids_ref[tile * per : tile * per + per, :] - base
        missed = jnp.where((ids >= head + SPAN) & (ids < tail), 1.0, missed)
    gaps[0] = jnp.max(missed).astype(jnp.int32)


def later_windows(ids_smem, base, tile, slots, gaps, use):
    head, tail, last = window_starts(ids_smem, base, tile, slots)

    @pl.when(last >= head + SPAN)
    def _():
        use(tail, jnp.maximum(tail, head + SPAN), tail + SPAN)

        @pl.when(gaps[0] > 0)
        def _():
            def step(n, carry):
                at = pl.multiple_of(head + (n + 1) * SPAN, 16)
                use(jnp.minimum(at, slots - SPAN), at, jnp.minimum(at + SPAN, tail))
                return carry

            count = (jnp.maximum(tail - head - SPAN, 0) + SPAN - 1) // SPAN
            lax.fori_loop(0, count, step, 0)


def sums_kernel(ids_smem, base_smem, ids_ref, points_ref, counts_ref, cent_ref, moved_ref, down_ref, up_ref, acc, gaps):
    base = base_smem[0]
    own = cent_ref.shape[0]
    slots = own + 2 * RIM
    per = TILE // 128

    @pl.when(pl.program_id(0) == 0)
    def _():
        note_gaps(ids_smem, ids_ref, base, slots, gaps)

    acc[...] = jnp.zeros_like(acc)

    for tile in range(points_ref.shape[0] // TILE):
        rows = slice(tile * TILE, tile * TILE + TILE)
        ids = jnp.concatenate([ids_ref[tile * per + k : tile * per + k + 1, :] for k in range(per)], axis=1) - base

        def add(start, low, high):
            start = pl.multiple_of(start, 16)
            slot = lax.broadcasted_iota(jnp.int32, (SPAN, TILE), 0) + start
            pick = ((slot == ids) & (ids >= low) & (ids < high)).astype(jnp.float32).astype(jnp.bfloat16)
            acc[pl.ds(start, SPAN), :] += jnp.dot(pick, points_ref[rows, :], preferred_element_type=jnp.float32)

        head, _, _ = window_starts(ids_smem, base, tile, slots)
        add(head, head, head + SPAN)
        later_windows(ids_smem, base, tile, slots, gaps, add)

    down_ref[...] = acc[:RIM].astype(jnp.bfloat16)
    up_ref[...] = acc[RIM + own :].astype(jnp.bfloat16)
    for part in range(own // 128):
        count = jnp.broadcast_to(counts_ref[part : part + 1, :], (128, 128)).astype(jnp.float32)
        inverse = (1.0 / (count + 2.0)).T
        lo = RIM if part == 0 else 0
        hi = 128 - RIM if part == own // 128 - 1 else 128
        at = slice(part * 128 + lo, part * 128 + hi)
        for col in range(COLS // 128):
            cols = slice(col * 128, col * 128 + 128)
            moved_ref[at, cols] = (
                acc[RIM + part * 128 + lo : RIM + part * 128 + hi, cols] + 2.0 * cent_ref[at, cols]
            ) * inverse[lo:hi]
    moved_ref[:RIM, :] = acc[RIM : 2 * RIM]
    moved_ref[own - RIM :, :] = acc[own : own + RIM]


def edge_kernel(moved_in, low_in, high_in, counts_ref, cent_ref, moved_ref):
    which = pl.program_id(0)
    row = jnp.where(which == 0, 0, counts_ref.shape[0] - 1)
    count = jnp.broadcast_to(counts_ref[pl.ds(row, 1), :], (128, 128)).astype(jnp.float32)
    inverse = (1.0 / (count + 2.0)).T
    inverse = jnp.where(which == 0, inverse[:RIM], inverse[RIM:])
    spread = jnp.where(which == 0, low_in[...].astype(jnp.float32), high_in[...].astype(jnp.float32))
    for col in range(cent_ref.shape[1] // 128):
        cols = slice(col * 128, col * 128 + 128)
        moved_ref[:, cols] = (moved_in[:, cols] + spread[:, cols] + 2.0 * cent_ref[:, cols]) * inverse


def quant_kernel(
    ids_smem, place_smem, ids_ref, points_ref, cent_ref, low_ref, high_ref, books_ref, *refs
):
    rebuilt_ref, payload_ref, hi_win, mid_win, lo_win, picks, ids_col, resid, books_low, norms, totals, mass, gaps = refs[-13:]
    base = place_smem[0]
    subs, codes, subdim = books_ref.shape
    rate = 1.0 / (math.sqrt(subdim) * math.log(2.0))
    own = cent_ref.shape[0]
    slots = own + 2 * RIM
    rows = points_ref.shape[0]
    tiles = rows // TILE
    lane = lax.broadcasted_iota(jnp.int32, (1, DEPTH), 1)
    pattern = jnp.where(lane < PIECES * SPAN, lax.rem(lane, SPAN), -1)

    def pick_rows(tile, start, low, high):
        ids = ids_col[tile * TILE : tile * TILE + TILE, :]
        ids = jnp.where((ids >= low) & (ids < high), ids - start, -2)
        parts = [(ids == pattern[:, k * 128 : k * 128 + 128]).astype(jnp.float32) for k in range(DEPTH // 128)]
        return jnp.concatenate(parts, axis=1).astype(jnp.bfloat16)

    def split(value, at):
        at = slice(at, at + value.shape[0])
        hi = value.astype(jnp.bfloat16)
        rest = value - hi.astype(jnp.float32)
        mid = rest.astype(jnp.bfloat16)
        hi_win[at] = hi
        mid_win[at] = mid
        lo_win[at] = (rest - mid.astype(jnp.float32)).astype(jnp.bfloat16)

    @pl.when(pl.program_id(0) == 0)
    def _():
        note_gaps(ids_smem, ids_ref, base, slots, gaps)
        for k in range(rows // 128):
            ids_col[k * 128 : k * 128 + 128, :] = jnp.broadcast_to(ids_ref[k : k + 1, :] - base, (128, 128)).T
        for tile in range(tiles):
            head, _, _ = window_starts(ids_smem, base, tile, slots)
            picks[tile] = pick_rows(tile, head, head, head + SPAN)

    split(low_ref[...], 0)
    split(cent_ref[...], RIM)
    split(high_ref[...], RIM + own)
    for j in range(subs):
        words = books_ref[j]
        books_low[j] = words.astype(jnp.bfloat16)
        norms[j] = jnp.broadcast_to(jnp.sum(words * words, axis=1, keepdims=True) * rate, (codes, 128))

    def fetch(pick, start):
        at = pl.ds(pl.multiple_of(start, 16), SPAN)
        rest = jnp.zeros((DEPTH - PIECES * SPAN, COLS), jnp.bfloat16)
        window = jnp.concatenate([hi_win[at, :], mid_win[at, :], lo_win[at, :], rest], axis=0)
        return jnp.dot(pick, window, preferred_element_type=jnp.float32)

    for tile in range(tiles):
        at = slice(tile * TILE, tile * TILE + TILE)
        head, _, _ = window_starts(ids_smem, base, tile, slots)
        resid[at, :] = (points_ref[at, :].astype(jnp.float32) - fetch(picks[tile], head)).astype(jnp.bfloat16)

    for tile in range(tiles):
        at = slice(tile * TILE, tile * TILE + TILE)

        def redo(start, low, high):
            got = fetch(pick_rows(tile, start, low, high), start)
            fresh = points_ref[at, :].astype(jnp.float32) - got
            ids = ids_col[at, :]
            new = (ids >= low) & (ids < high)
            for k in range(COLS // 128):
                cols = slice(k * 128, k * 128 + 128)
                resid[at, cols] = jnp.where(new, fresh[:, cols], resid[at, cols].astype(jnp.float32)).astype(jnp.bfloat16)

        later_windows(ids_smem, base, tile, slots, gaps, redo)

    units = [(j, c) for j in range(subs) for c in range(rows // CHUNK)]

    def place(unit):
        j, c = unit
        return slice(c * CHUNK, c * CHUNK + CHUNK), slice(j * subdim, j * subdim + subdim)

    def dots_of(unit):
        return lax.dot_general(books_low[unit[0]], resid[place(unit)], NT, preferred_element_type=jnp.float32)

    def weigh(unit, dots):
        j, c = unit
        low, over_rows = [], None
        for part in range(CHUNK // 128):
            logits = dots[:, part * 128 : part * 128 + 128] * (2.0 * rate) - norms[j]
            top = jnp.max(logits, axis=0, keepdims=True)
            raised = jnp.exp2(logits - top)
            weights = raised * (1.0 / jnp.sum(raised, axis=0, keepdims=True))
            low.append(weights.astype(jnp.bfloat16))
            over_rows = weights if over_rows is None else over_rows + weights
        mass[j] = over_rows if c == 0 else mass[j] + over_rows
        return jnp.concatenate(low, axis=1)

    def products(unit, weights_low):
        j, c = unit
        got = jnp.dot(weights_low, resid[place(unit)], preferred_element_type=jnp.float32)
        totals[j] = got if c == 0 else totals[j] + got
        rebuilt = lax.dot_general(weights_low, books_low[j], TN, preferred_element_type=jnp.float32)
        rebuilt_ref[place(unit)] = rebuilt.astype(jnp.bfloat16)

    dots, weights_low = dots_of(units[0]), None
    for n, unit in enumerate(units):
        ahead = dots_of(units[n + 1]) if n + 1 < len(units) else None
        fresh = weigh(unit, dots)
        if n > 0:
            products(units[n - 1], weights_low)
        dots, weights_low = ahead, fresh
    products(units[-1], weights_low)

    group = payload_ref.shape[1] - 8
    left = lax.broadcasted_iota(jnp.int32, (8, 128), 1) < 64
    for j in range(subs):
        for g in range(codes // group):
            at = slice(g * group, g * group + group)
            slot = j * (codes // group) + g
            payload_ref[slot, :group, :] = totals[j, at, :]
            part = mass[j, at, :]
            part = part + pltpu.roll(part, 64, 1)
            payload_ref[slot, group:, :] = jnp.where(left, part[:8], part[8:])


def reduce_kernel(prior, parts_ref, book_ref, out_ref):
    total = jnp.sum(parts_ref[...], axis=0)
    group = book_ref.shape[0]
    left = lax.broadcasted_iota(jnp.int32, (8, 128), 1) < 64
    packed = total[group:]
    mass = jnp.concatenate(
        [
            jnp.sum(jnp.where(left, packed, 0.0), axis=1, keepdims=True),
            jnp.sum(jnp.where(left, 0.0, packed), axis=1, keepdims=True),
        ],
        axis=0,
    )
    moved = (total[:group] + prior * book_ref[...]) / (mass + prior)
    out_ref[...] = jnp.broadcast_to(moved[None], out_ref.shape)


def whole(shape):
    return pl.BlockSpec(shape, lambda *_: (0,) * len(shape))


def quantize(assign, place, ids, points, centroids, low, high, books, owners, rebuilt):
    rows_here, width = points.shape
    half, codes, subdim = books.shape
    own = centroids.shape[0]
    subs = COLS // subdim
    steps = half // subs
    group = half * codes // owners
    slots = own + 2 * RIM

    def columns(count):
        return pl.BlockSpec((count, COLS), lambda i, ids, place: (0, place[1] + i))

    in_specs = [
        whole(ids.shape), columns(rows_here), columns(own), columns(RIM), columns(RIM),
        pl.BlockSpec((subs, codes, subdim), lambda i, *_: (i, 0, 0)),
    ]
    inputs = [assign, place, ids, points, centroids, low, high, books]
    aliases = {}
    if rebuilt is not None:
        aliases = {len(inputs): 0}
        in_specs.append(pl.BlockSpec(memory_space=pl.ANY))
        inputs.append(rebuilt)
    return pl.pallas_call(
        quant_kernel,
        grid_spec=pltpu.PrefetchScalarGridSpec(
            num_scalar_prefetch=2,
            grid=(steps,),
            in_specs=in_specs,
            out_specs=[columns(rows_here), pl.BlockSpec((owners // steps, group + 8, subdim), lambda i, *_: (i, 0, 0))],
            scratch_shapes=[pltpu.VMEM((slots, COLS), jnp.bfloat16)] * 3
            + [
                pltpu.VMEM((rows_here // TILE, TILE, DEPTH), jnp.bfloat16),
                pltpu.VMEM((rows_here, 128), jnp.int32),
                pltpu.VMEM((rows_here, COLS), jnp.bfloat16),
                pltpu.VMEM((subs, codes, subdim), jnp.bfloat16),
                pltpu.VMEM((subs, codes, 128), jnp.float32),
                pltpu.VMEM((subs, codes, subdim), jnp.float32),
                pltpu.VMEM((subs, codes, 128), jnp.float32),
                pltpu.SMEM((1,), jnp.int32),
            ],
        ),
        out_shape=[
            jax.ShapeDtypeStruct(points.shape, jnp.bfloat16),
            jax.ShapeDtypeStruct((owners, group + 8, subdim), jnp.float32),
        ],
        input_output_aliases=aliases,
        compiler_params=pltpu.CompilerParams(vmem_limit_bytes=58 * 1024 * 1024),
        cost_estimate=pl.CostEstimate(flops=4 * 10**9, bytes_accessed=6 * 10**6, transcendentals=2 * 10**6),
        name="quantize",
    )(*inputs)


def cluster_sums(assign, place, ids, points, counts, centroids):
    rows_here, width = points.shape
    own = centroids.shape[0]

    def columns(count):
        return pl.BlockSpec((count, COLS), lambda i, *_: (0, i))

    return pl.pallas_call(
        sums_kernel,
        grid_spec=pltpu.PrefetchScalarGridSpec(
            num_scalar_prefetch=2,
            grid=(width // COLS,),
            in_specs=[whole(ids.shape), columns(rows_here), whole(counts.shape), columns(own)],
            out_specs=[columns(own), columns(RIM), columns(RIM)],
            scratch_shapes=[pltpu.VMEM((own + 2 * RIM, COLS), jnp.float32), pltpu.SMEM((1,), jnp.int32)],
        ),
        out_shape=[
            jax.ShapeDtypeStruct(centroids.shape, jnp.float32),
            jax.ShapeDtypeStruct((RIM, width), jnp.bfloat16),
            jax.ShapeDtypeStruct((RIM, width), jnp.bfloat16),
        ],
        compiler_params=pltpu.CompilerParams(vmem_limit_bytes=58 * 1024 * 1024),
        cost_estimate=pl.CostEstimate(flops=2 * 10**9, bytes_accessed=8 * 10**6, transcendentals=0),
        name="cluster_sums",
    )(assign, place, ids, points, counts, centroids)


def body(points, assign, cluster_counts, centroids, codebook):
    own, width = centroids.shape
    rows_here = points.shape[0]
    half, codes, subdim = codebook.shape
    rows_axis, sub_axis = MESH_AXES
    owners = lax.axis_size(rows_axis)
    places = owners * lax.axis_size(sub_axis)
    sub = lax.axis_index(sub_axis)
    position = lax.axis_index(rows_axis) * lax.axis_size(sub_axis) + sub
    base = position * own - RIM
    blocks = half * subdim // COLS
    up = [(i, i + 1) for i in range(places - 1)]
    down = [(i + 1, i) for i in range(places - 1)]
    swap = [(0, 1), (1, 0)]
    other_book = lax.ppermute(codebook, sub_axis, swap)
    low = lax.ppermute(centroids[own - RIM :], MESH_AXES, up)
    high = lax.ppermute(centroids[:RIM], MESH_AXES, down)
    ids = assign.reshape(rows_here // 128, 128)
    counts = cluster_counts.reshape(own // 128, 128)
    group = half * codes // owners

    theirs = jnp.stack([base, (1 - sub) * blocks]).astype(jnp.int32)
    mine = jnp.stack([base, sub * blocks]).astype(jnp.int32)
    rebuilt, away = quantize(assign, theirs, ids, points, centroids, low, high, other_book, owners, None)
    arrived = lax.ppermute(away, sub_axis, swap)
    rebuilt, kept = quantize(assign, mine, ids, points, centroids, low, high, codebook, owners, rebuilt)

    parts = lax.all_to_all(kept + arrived, rows_axis, 0, 0, tiled=True)
    later = lax.optimization_barrier((mine, kept))[0]
    sums, sum_down, sum_up = cluster_sums(assign, later, ids, points, counts, centroids)
    parts, sum_down, sum_up = lax.optimization_barrier((parts, sum_down, sum_up))
    sum_low = lax.ppermute(sum_up, MESH_AXES, up)
    sum_high = lax.ppermute(sum_down, MESH_AXES, down)

    book_rows = lax.dynamic_slice_in_dim(
        codebook.reshape(half * codes, subdim), lax.axis_index(rows_axis) * group, group, 0
    )
    prior = rows_here * places / codes
    moved = pl.pallas_call(
        functools.partial(reduce_kernel, prior),
        out_shape=jax.ShapeDtypeStruct((owners, group, subdim), jnp.float32),
        compiler_params=pltpu.CompilerParams(vmem_limit_bytes=8 * 1024 * 1024),
        name="moved_codes",
    )(parts, book_rows)
    moved = lax.all_to_all(moved, rows_axis, 0, 0, tiled=True)

    edge = pl.BlockSpec((RIM, width), lambda i: (i * (own // RIM - 1), 0))
    moved_centroids = pl.pallas_call(
        edge_kernel,
        grid=(2,),
        in_specs=[edge, whole((RIM, width)), whole((RIM, width)), whole(counts.shape), edge],
        out_specs=edge,
        out_shape=jax.ShapeDtypeStruct(centroids.shape, jnp.float32),
        input_output_aliases={0: 0},
        compiler_params=pltpu.CompilerParams(vmem_limit_bytes=8 * 1024 * 1024),
        name="edge_clusters",
    )(sums, sum_low, sum_high, counts, centroids)
    return (rebuilt, moved_centroids, moved.reshape(codebook.shape))


def solution(mesh):
    both = P(("rows", "sub"), None)
    flat = P(("rows", "sub"))
    books = P("sub", None, None)
    return jax.shard_map(
        body,
        mesh=mesh,
        in_specs=(both, flat, flat, both, books),
        out_specs=(both, both, books),
        check_vma=False,
    )
```

```python
import functools
import math

import jax
import jax.numpy as jnp
from jax import lax
from jax.experimental import pallas as pl
from jax.experimental.pallas import tpu as pltpu
from jax.sharding import PartitionSpec as P

RIM = 64
TILE = 256
CHUNK = 512
COLS = 256
SPAN = 80
PIECES = 3
DEPTH = 256
MESH_AXES = ("rows", "sub")
NT = (((1,), (1,)), ((), ()))
TN = (((0,), (0,)), ((), ()))


def window_starts(ids_smem, base, tile, slots):
    first = ids_smem[tile * TILE] - base
    last = ids_smem[tile * TILE + TILE - 1] - base
    head = jnp.minimum((first // 16) * 16, slots - SPAN)
    tail = jnp.clip((last // 16) * 16 - (SPAN - 16), 0, slots - SPAN)
    return pl.multiple_of(head, 16), pl.multiple_of(tail, 16), last


def note_gaps(ids_smem, ids_ref, base, slots, gaps):
    per = TILE // 128
    missed = jnp.zeros((per, 128), jnp.float32)
    for tile in range(ids_ref.shape[0] // per):
        head, tail, _ = window_starts(ids_smem, base, tile, slots)
        ids = ids_ref[tile * per : tile * per + per, :] - base
        missed = jnp.where((ids >= head + SPAN) & (ids < tail), 1.0, missed)
    gaps[0] = jnp.max(missed).astype(jnp.int32)


def middle_windows(ids_smem, base, tile, slots, use):
    head, tail, _ = window_starts(ids_smem, base, tile, slots)

    def step(n, carry):
        at = pl.multiple_of(head + (n + 1) * SPAN, 16)
        use(jnp.minimum(at, slots - SPAN), at, jnp.minimum(at + SPAN, tail))
        return carry

    count = (jnp.maximum(tail - head - SPAN, 0) + SPAN - 1) // SPAN
    lax.fori_loop(0, count, step, 0)


def sums_kernel(
    ids_smem, place_smem, ids_ref, points_ref, counts_ref, cent_ref, moved_ref, inner_ref, outer_ref, acc, picks, gaps
):
    base = place_smem[0]
    own = cent_ref.shape[0]
    slots = own + 2 * RIM
    per = TILE // 128
    tiles = points_ref.shape[0] // TILE

    def pick_slots(tile, start, low, high):
        ids = jnp.concatenate([ids_ref[tile * per + k : tile * per + k + 1, :] for k in range(per)], axis=1) - base
        ids = jnp.where((ids >= low) & (ids < high), ids - start, -1)
        slot = lax.broadcasted_iota(jnp.int32, (SPAN, TILE), 0)
        return (slot == ids).astype(jnp.float32).astype(jnp.bfloat16)

    @pl.when(pl.program_id(0) == 0)
    def _():
        note_gaps(ids_smem, ids_ref, base, slots, gaps)
        for tile in range(tiles):
            head, tail, _ = window_starts(ids_smem, base, tile, slots)
            picks[tile, :SPAN] = pick_slots(tile, head, head, head + SPAN)
            picks[tile, SPAN:] = pick_slots(tile, tail, jnp.maximum(tail, head + SPAN), tail + SPAN)

    acc[...] = jnp.zeros_like(acc)
    sums = [
        jnp.dot(picks[tile], points_ref[tile * TILE : tile * TILE + TILE, :], preferred_element_type=jnp.float32)
        for tile in range(tiles)
    ]
    for tile in range(tiles):
        head, tail, _ = window_starts(ids_smem, base, tile, slots)
        acc[pl.ds(head, SPAN), :] += sums[tile][:SPAN]
        acc[pl.ds(tail, SPAN), :] += sums[tile][SPAN:]

    @pl.when(gaps[0] > 0)
    def _():
        for tile in range(tiles):
            rows = slice(tile * TILE, tile * TILE + TILE)

            def add(start, low, high):
                start = pl.multiple_of(start, 16)
                pick = pick_slots(tile, start, low, high)
                acc[pl.ds(start, SPAN), :] += jnp.dot(pick, points_ref[rows, :], preferred_element_type=jnp.float32)

            middle_windows(ids_smem, base, tile, slots, add)

    down = acc[:RIM].astype(jnp.bfloat16)
    up = acc[RIM + own :].astype(jnp.bfloat16)
    first = place_smem[2] == 0
    inner_ref[...] = jnp.where(first, up, down)
    outer_ref[...] = jnp.where(first, down, up)
    for part in range(own // 128):
        count = jnp.broadcast_to(counts_ref[part : part + 1, :], (128, 128)).astype(jnp.float32)
        inverse = (1.0 / (count + 2.0)).T
        lo = RIM if part == 0 else 0
        hi = 128 - RIM if part == own // 128 - 1 else 128
        at = slice(part * 128 + lo, part * 128 + hi)
        for col in range(COLS // 128):
            cols = slice(col * 128, col * 128 + 128)
            moved_ref[at, cols] = (
                acc[RIM + part * 128 + lo : RIM + part * 128 + hi, cols] + 2.0 * cent_ref[at, cols]
            ) * inverse[lo:hi]
    moved_ref[:RIM, :] = acc[RIM : 2 * RIM]
    moved_ref[own - RIM :, :] = acc[own : own + RIM]


def edge_kernel(place_smem, moved_in, inner_in, outer_in, counts_ref, cent_ref, moved_ref):
    which = pl.program_id(0)
    row = jnp.where(which == 0, 0, counts_ref.shape[0] - 1)
    count = jnp.broadcast_to(counts_ref[pl.ds(row, 1), :], (128, 128)).astype(jnp.float32)
    inverse = (1.0 / (count + 2.0)).T
    inverse = jnp.where(which == 0, inverse[:RIM], inverse[RIM:])
    outer = which == place_smem[2]
    spread = jnp.where(outer, outer_in[...].astype(jnp.float32), inner_in[...].astype(jnp.float32))
    for col in range(cent_ref.shape[1] // 128):
        cols = slice(col * 128, col * 128 + 128)
        moved_ref[:, cols] = (moved_in[:, cols] + spread[:, cols] + 2.0 * cent_ref[:, cols]) * inverse


def quant_kernel(
    ids_smem, place_smem, ids_ref, points_ref, cent_ref, inner_ref, outer_ref, books_ref, *refs
):
    rebuilt_ref, payload_ref, hi_win, mid_win, lo_win, picks, ids_col, resid, books_low, norms, totals, mass, gaps = refs[-13:]
    base = place_smem[0]
    subs, codes, subdim = books_ref.shape
    rate = 1.0 / (math.sqrt(subdim) * math.log(2.0))
    own = cent_ref.shape[0]
    slots = own + 2 * RIM
    rows = points_ref.shape[0]
    tiles = rows // TILE
    lane = lax.broadcasted_iota(jnp.int32, (1, DEPTH), 1)
    pattern = jnp.where(lane < PIECES * SPAN, lax.rem(lane, SPAN), -1)

    def pick_rows(tile, start, low, high):
        ids = ids_col[tile * TILE : tile * TILE + TILE, :]
        ids = jnp.where((ids >= low) & (ids < high), ids - start, -2)
        parts = [(ids == pattern[:, k * 128 : k * 128 + 128]).astype(jnp.float32) for k in range(DEPTH // 128)]
        return jnp.concatenate(parts, axis=1).astype(jnp.bfloat16)

    def split(value, at):
        at = slice(at, at + value.shape[0])
        hi = value.astype(jnp.bfloat16)
        rest = value - hi.astype(jnp.float32)
        mid = rest.astype(jnp.bfloat16)
        hi_win[at] = hi
        mid_win[at] = mid
        lo_win[at] = (rest - mid.astype(jnp.float32)).astype(jnp.bfloat16)

    @pl.when(pl.program_id(0) == 0)
    def _():
        note_gaps(ids_smem, ids_ref, base, slots, gaps)
        for k in range(rows // 128):
            ids_col[k * 128 : k * 128 + 128, :] = jnp.broadcast_to(ids_ref[k : k + 1, :] - base, (128, 128)).T
        for tile in range(tiles):
            head, tail, _ = window_starts(ids_smem, base, tile, slots)
            picks[tile, :, :DEPTH] = pick_rows(tile, head, head, head + SPAN)
            picks[tile, :, DEPTH:] = pick_rows(tile, tail, jnp.maximum(tail, head + SPAN), tail + SPAN)

    first = place_smem[2] == 0
    split(jnp.where(first, outer_ref[...], inner_ref[...]), 0)
    split(cent_ref[...], RIM)
    split(jnp.where(first, inner_ref[...], outer_ref[...]), RIM + own)
    for j in range(subs):
        words = books_ref[j]
        books_low[j] = words.astype(jnp.bfloat16)
        norms[j] = jnp.broadcast_to(jnp.sum(words * words, axis=1, keepdims=True) * rate, (codes, 128))

    def window(start):
        at = pl.ds(pl.multiple_of(start, 16), SPAN)
        rest = jnp.zeros((DEPTH - PIECES * SPAN, COLS), jnp.bfloat16)
        return [hi_win[at, :], mid_win[at, :], lo_win[at, :], rest]

    def subtract(tile):
        at = slice(tile * TILE, tile * TILE + TILE)
        head, tail, _ = window_starts(ids_smem, base, tile, slots)
        both = jnp.concatenate(window(head) + window(tail), axis=0)
        got = jnp.dot(picks[tile], both, preferred_element_type=jnp.float32)
        resid[at, :] = (points_ref[at, :].astype(jnp.float32) - got).astype(jnp.bfloat16)

    for tile in range(tiles):
        subtract(tile)

    @pl.when(gaps[0] > 0)
    def _():
        for tile in range(tiles):
            at = slice(tile * TILE, tile * TILE + TILE)

            def redo(start, low, high):
                pick = pick_rows(tile, start, low, high)
                got = jnp.dot(pick, jnp.concatenate(window(start), axis=0), preferred_element_type=jnp.float32)
                fresh = points_ref[at, :].astype(jnp.float32) - got
                ids = ids_col[at, :]
                new = (ids >= low) & (ids < high)
                for k in range(COLS // 128):
                    cols = slice(k * 128, k * 128 + 128)
                    kept = resid[at, cols].astype(jnp.float32)
                    resid[at, cols] = jnp.where(new, fresh[:, cols], kept).astype(jnp.bfloat16)

            middle_windows(ids_smem, base, tile, slots, redo)

    units = [(j, c) for j in range(subs) for c in range(rows // CHUNK)]

    def place(unit):
        j, c = unit
        return slice(c * CHUNK, c * CHUNK + CHUNK), slice(j * subdim, j * subdim + subdim)

    def dots_of(unit):
        return lax.dot_general(books_low[unit[0]], resid[place(unit)], NT, preferred_element_type=jnp.float32)

    def weigh(unit, dots):
        j, c = unit
        low, over_rows = [], None
        for part in range(CHUNK // 128):
            logits = dots[:, part * 128 : part * 128 + 128] * (2.0 * rate) - norms[j]
            top = jnp.max(logits, axis=0, keepdims=True)
            raised = jnp.exp2(logits - top)
            weights = raised * (1.0 / jnp.sum(raised, axis=0, keepdims=True))
            low.append(weights.astype(jnp.bfloat16))
            over_rows = weights if over_rows is None else over_rows + weights
        mass[j] = over_rows if c == 0 else mass[j] + over_rows
        return jnp.concatenate(low, axis=1)

    def products(unit, weights_low):
        j, c = unit
        got = jnp.dot(weights_low, resid[place(unit)], preferred_element_type=jnp.float32)
        totals[j] = got if c == 0 else totals[j] + got
        rebuilt = lax.dot_general(weights_low, books_low[j], TN, preferred_element_type=jnp.float32)
        rebuilt_ref[place(unit)] = rebuilt.astype(jnp.bfloat16)

    dots, weights_low = dots_of(units[0]), None
    for n, unit in enumerate(units):
        ahead = dots_of(units[n + 1]) if n + 1 < len(units) else None
        fresh = weigh(unit, dots)
        if n > 0:
            products(units[n - 1], weights_low)
        dots, weights_low = ahead, fresh
    products(units[-1], weights_low)

    group = payload_ref.shape[1] - 8
    left = lax.broadcasted_iota(jnp.int32, (8, 128), 1) < 64
    for j in range(subs):
        for g in range(codes // group):
            at = slice(g * group, g * group + group)
            slot = j * (codes // group) + g
            payload_ref[slot, :group, :] = totals[j, at, :]
            part = mass[j, at, :]
            part = part + pltpu.roll(part, 64, 1)
            payload_ref[slot, group:, :] = jnp.where(left, part[:8], part[8:])


def reduce_kernel(prior, parts_ref, book_ref, out_ref):
    total = jnp.sum(parts_ref[...], axis=0)
    group = book_ref.shape[0]
    left = lax.broadcasted_iota(jnp.int32, (8, 128), 1) < 64
    packed = total[group:]
    mass = jnp.concatenate(
        [
            jnp.sum(jnp.where(left, packed, 0.0), axis=1, keepdims=True),
            jnp.sum(jnp.where(left, 0.0, packed), axis=1, keepdims=True),
        ],
        axis=0,
    )
    moved = (total[:group] + prior * book_ref[...]) / (mass + prior)
    out_ref[...] = jnp.broadcast_to(moved[None], out_ref.shape)


def whole(shape):
    return pl.BlockSpec(shape, lambda *_: (0,) * len(shape))


def quantize(assign, place, ids, points, centroids, inner, outer, books, owners, rebuilt):
    rows_here, width = points.shape
    half, codes, subdim = books.shape
    own = centroids.shape[0]
    subs = COLS // subdim
    steps = half // subs
    group = half * codes // owners
    slots = own + 2 * RIM

    def columns(count):
        return pl.BlockSpec((count, COLS), lambda i, ids, place: (0, place[1] + i))

    in_specs = [
        whole(ids.shape), columns(rows_here), columns(own), columns(RIM), columns(RIM),
        pl.BlockSpec((subs, codes, subdim), lambda i, *_: (i, 0, 0)),
    ]
    inputs = [assign, place, ids, points, centroids, inner, outer, books]
    aliases = {}
    if rebuilt is not None:
        aliases = {len(inputs): 0}
        in_specs.append(pl.BlockSpec(memory_space=pl.ANY))
        inputs.append(rebuilt)
    return pl.pallas_call(
        quant_kernel,
        grid_spec=pltpu.PrefetchScalarGridSpec(
            num_scalar_prefetch=2,
            grid=(steps,),
            in_specs=in_specs,
            out_specs=[columns(rows_here), pl.BlockSpec((owners // steps, group + 8, subdim), lambda i, *_: (i, 0, 0))],
            scratch_shapes=[pltpu.VMEM((slots, COLS), jnp.bfloat16)] * 3
            + [
                pltpu.VMEM((rows_here // TILE, TILE, 2 * DEPTH), jnp.bfloat16),
                pltpu.VMEM((rows_here, 128), jnp.int32),
                pltpu.VMEM((rows_here, COLS), jnp.bfloat16),
                pltpu.VMEM((subs, codes, subdim), jnp.bfloat16),
                pltpu.VMEM((subs, codes, 128), jnp.float32),
                pltpu.VMEM((subs, codes, subdim), jnp.float32),
                pltpu.VMEM((subs, codes, 128), jnp.float32),
                pltpu.SMEM((1,), jnp.int32),
            ],
        ),
        out_shape=[
            jax.ShapeDtypeStruct(points.shape, jnp.bfloat16),
            jax.ShapeDtypeStruct((owners, group + 8, subdim), jnp.float32),
        ],
        input_output_aliases=aliases,
        compiler_params=pltpu.CompilerParams(vmem_limit_bytes=58 * 1024 * 1024),
        cost_estimate=pl.CostEstimate(flops=4 * 10**9, bytes_accessed=6 * 10**6, transcendentals=2 * 10**6),
        name="quantize",
    )(*inputs)


def cluster_sums(assign, place, ids, points, counts, centroids):
    rows_here, width = points.shape
    own = centroids.shape[0]

    def columns(count):
        return pl.BlockSpec((count, COLS), lambda i, *_: (0, i))

    return pl.pallas_call(
        sums_kernel,
        grid_spec=pltpu.PrefetchScalarGridSpec(
            num_scalar_prefetch=2,
            grid=(width // COLS,),
            in_specs=[whole(ids.shape), columns(rows_here), whole(counts.shape), columns(own)],
            out_specs=[columns(own), columns(RIM), columns(RIM)],
            scratch_shapes=[
                pltpu.VMEM((own + 2 * RIM, COLS), jnp.float32),
                pltpu.VMEM((rows_here // TILE, 2 * SPAN, TILE), jnp.bfloat16),
                pltpu.SMEM((1,), jnp.int32),
            ],
        ),
        out_shape=[
            jax.ShapeDtypeStruct(centroids.shape, jnp.float32),
            jax.ShapeDtypeStruct((RIM, width), jnp.bfloat16),
            jax.ShapeDtypeStruct((RIM, width), jnp.bfloat16),
        ],
        compiler_params=pltpu.CompilerParams(vmem_limit_bytes=58 * 1024 * 1024),
        cost_estimate=pl.CostEstimate(flops=2 * 10**9, bytes_accessed=8 * 10**6, transcendentals=0),
        name="cluster_sums",
    )(assign, place, ids, points, counts, centroids)


def body(points, assign, cluster_counts, centroids, codebook):
    own, width = centroids.shape
    rows_here = points.shape[0]
    half, codes, subdim = codebook.shape
    rows_axis, sub_axis = MESH_AXES
    owners = lax.axis_size(rows_axis)
    places = owners * lax.axis_size(sub_axis)
    sub = lax.axis_index(sub_axis)
    position = lax.axis_index(rows_axis) * lax.axis_size(sub_axis) + sub
    base = position * own - RIM
    blocks = half * subdim // COLS
    swap = [(0, 1), (1, 0)]
    pairs = [(i, i + 1) for i in range(1, places - 1, 2)]
    across = pairs + [(j, i) for i, j in pairs]
    other_book = lax.ppermute(codebook, sub_axis, swap)
    outer = lax.dynamic_slice_in_dim(centroids, sub * (own - RIM), RIM, 0)
    inner = lax.dynamic_slice_in_dim(centroids, (1 - sub) * (own - RIM), RIM, 0)
    outer = lax.ppermute(outer, MESH_AXES, across)
    inner = lax.ppermute(inner, sub_axis, swap)
    ids = assign.reshape(rows_here // 128, 128)
    counts = cluster_counts.reshape(own // 128, 128)
    group = half * codes // owners

    theirs = jnp.stack([base, (1 - sub) * blocks, sub]).astype(jnp.int32)
    mine = jnp.stack([base, sub * blocks, sub]).astype(jnp.int32)
    rebuilt, away = quantize(assign, theirs, ids, points, centroids, inner, outer, other_book, owners, None)
    arrived = lax.ppermute(away, sub_axis, swap)
    rebuilt, kept = quantize(assign, mine, ids, points, centroids, inner, outer, codebook, owners, rebuilt)

    parts = lax.all_to_all(kept + arrived, rows_axis, 0, 0, tiled=True)
    later = lax.optimization_barrier((mine, kept))[0]
    sums, sum_inner, sum_outer = cluster_sums(assign, later, ids, points, counts, centroids)
    sum_outer = lax.ppermute(sum_outer, MESH_AXES, across)
    sum_inner = lax.ppermute(sum_inner, sub_axis, swap)
    parts, sum_inner, sum_outer = lax.optimization_barrier((parts, sum_inner, sum_outer))

    book_rows = lax.dynamic_slice_in_dim(
        codebook.reshape(half * codes, subdim), lax.axis_index(rows_axis) * group, group, 0
    )
    prior = rows_here * places / codes
    moved = pl.pallas_call(
        functools.partial(reduce_kernel, prior),
        out_shape=jax.ShapeDtypeStruct((owners, group, subdim), jnp.float32),
        compiler_params=pltpu.CompilerParams(vmem_limit_bytes=8 * 1024 * 1024),
        name="moved_codes",
    )(parts, book_rows)
    moved = lax.all_to_all(moved, rows_axis, 0, 0, tiled=True)

    edge = pl.BlockSpec((RIM, width), lambda i, *_: (i * (own // RIM - 1), 0))
    moved_centroids = pl.pallas_call(
        edge_kernel,
        grid_spec=pltpu.PrefetchScalarGridSpec(
            num_scalar_prefetch=1,
            grid=(2,),
            in_specs=[edge, whole((RIM, width)), whole((RIM, width)), whole(counts.shape), edge],
            out_specs=edge,
        ),
        out_shape=jax.ShapeDtypeStruct(centroids.shape, jnp.float32),
        input_output_aliases={1: 0},
        compiler_params=pltpu.CompilerParams(vmem_limit_bytes=8 * 1024 * 1024),
        name="edge_clusters",
    )(mine, sums, sum_inner, sum_outer, counts, centroids)
    return (rebuilt, moved_centroids, moved.reshape(codebook.shape))


def solution(mesh):
    both = P(("rows", "sub"), None)
    flat = P(("rows", "sub"))
    books = P("sub", None, None)
    return jax.shard_map(
        body,
        mesh=mesh,
        in_specs=(both, flat, flat, both, books),
        out_specs=(both, both, books),
        check_vma=False,
    )
```

```python
import functools
import math

import jax
import jax.numpy as jnp
from jax import lax
from jax.experimental import pallas as pl
from jax.experimental.pallas import tpu as pltpu
from jax.sharding import PartitionSpec as P

RIM = 64
TILE = 256
CHUNK = 512
COLS = 256
SPAN = 80
PIECES = 3
DEPTH = 256
MESH_AXES = ("rows", "sub")
NT = (((1,), (1,)), ((), ()))
TN = (((0,), (0,)), ((), ()))


def window_starts(ids_smem, base, tile, slots):
    first = ids_smem[tile * TILE] - base
    last = ids_smem[tile * TILE + TILE - 1] - base
    head = jnp.minimum((first // 16) * 16, slots - SPAN)
    tail = jnp.clip((last // 16) * 16 - (SPAN - 16), 0, slots - SPAN)
    return pl.multiple_of(head, 16), pl.multiple_of(tail, 16), last


def note_gaps(ids_smem, ids_ref, base, slots, gaps):
    per = TILE // 128
    missed = jnp.zeros((per, 128), jnp.float32)
    for tile in range(ids_ref.shape[0] // per):
        head, tail, _ = window_starts(ids_smem, base, tile, slots)
        ids = ids_ref[tile * per : tile * per + per, :] - base
        missed = jnp.where((ids >= head + SPAN) & (ids < tail), 1.0, missed)
    gaps[0] = jnp.max(missed).astype(jnp.int32)


def middle_windows(ids_smem, base, tile, slots, use):
    head, tail, _ = window_starts(ids_smem, base, tile, slots)

    def step(n, carry):
        at = pl.multiple_of(head + (n + 1) * SPAN, 16)
        use(jnp.minimum(at, slots - SPAN), at, jnp.minimum(at + SPAN, tail))
        return carry

    count = (jnp.maximum(tail - head - SPAN, 0) + SPAN - 1) // SPAN
    lax.fori_loop(0, count, step, 0)


def sums_kernel(
    ids_smem, place_smem, ids_ref, points_ref, counts_ref, cent_ref, moved_ref, inner_ref, outer_ref, acc, picks, gaps
):
    base = place_smem[0]
    own = cent_ref.shape[0]
    slots = own + 2 * RIM
    per = TILE // 128
    tiles = points_ref.shape[0] // TILE

    def pick_slots(tile, start, low, high):
        ids = jnp.concatenate([ids_ref[tile * per + k : tile * per + k + 1, :] for k in range(per)], axis=1) - base
        ids = jnp.where((ids >= low) & (ids < high), ids - start, -1)
        slot = lax.broadcasted_iota(jnp.int32, (SPAN, TILE), 0)
        return (slot == ids).astype(jnp.float32).astype(jnp.bfloat16)

    @pl.when(pl.program_id(0) == 0)
    def _():
        note_gaps(ids_smem, ids_ref, base, slots, gaps)
        for tile in range(tiles):
            head, tail, _ = window_starts(ids_smem, base, tile, slots)
            picks[tile, :SPAN] = pick_slots(tile, head, head, head + SPAN)
            picks[tile, SPAN:] = pick_slots(tile, tail, jnp.maximum(tail, head + SPAN), tail + SPAN)

    acc[...] = jnp.zeros_like(acc)
    sums = [
        jnp.dot(picks[tile], points_ref[tile * TILE : tile * TILE + TILE, :], preferred_element_type=jnp.float32)
        for tile in range(tiles)
    ]
    for tile in range(tiles):
        head, tail, _ = window_starts(ids_smem, base, tile, slots)
        acc[pl.ds(head, SPAN), :] += sums[tile][:SPAN]
        acc[pl.ds(tail, SPAN), :] += sums[tile][SPAN:]

    @pl.when(gaps[0] > 0)
    def _():
        for tile in range(tiles):
            rows = slice(tile * TILE, tile * TILE + TILE)

            def add(start, low, high):
                start = pl.multiple_of(start, 16)
                pick = pick_slots(tile, start, low, high)
                acc[pl.ds(start, SPAN), :] += jnp.dot(pick, points_ref[rows, :], preferred_element_type=jnp.float32)

            middle_windows(ids_smem, base, tile, slots, add)

    down = acc[:RIM].astype(jnp.bfloat16)
    up = acc[RIM + own :].astype(jnp.bfloat16)
    first = place_smem[2] == 0
    inner_ref[...] = jnp.where(first, up, down)
    outer_ref[...] = jnp.where(first, down, up)
    for part in range(own // 128):
        count = jnp.broadcast_to(counts_ref[part : part + 1, :], (128, 128)).astype(jnp.float32)
        inverse = (1.0 / (count + 2.0)).T
        lo = RIM if part == 0 else 0
        hi = 128 - RIM if part == own // 128 - 1 else 128
        at = slice(part * 128 + lo, part * 128 + hi)
        for col in range(COLS // 128):
            cols = slice(col * 128, col * 128 + 128)
            moved_ref[at, cols] = (
                acc[RIM + part * 128 + lo : RIM + part * 128 + hi, cols] + 2.0 * cent_ref[at, cols]
            ) * inverse[lo:hi]
    moved_ref[:RIM, :] = acc[RIM : 2 * RIM]
    moved_ref[own - RIM :, :] = acc[own : own + RIM]


def edge_kernel(place_smem, moved_in, inner_in, outer_in, counts_ref, cent_ref, moved_ref):
    which = pl.program_id(0)
    row = jnp.where(which == 0, 0, counts_ref.shape[0] - 1)
    count = jnp.broadcast_to(counts_ref[pl.ds(row, 1), :], (128, 128)).astype(jnp.float32)
    inverse = (1.0 / (count + 2.0)).T
    inverse = jnp.where(which == 0, inverse[:RIM], inverse[RIM:])
    outer = which == place_smem[2]
    spread = jnp.where(outer, outer_in[...].astype(jnp.float32), inner_in[...].astype(jnp.float32))
    for col in range(cent_ref.shape[1] // 128):
        cols = slice(col * 128, col * 128 + 128)
        moved_ref[:, cols] = (moved_in[:, cols] + spread[:, cols] + 2.0 * cent_ref[:, cols]) * inverse


def quant_kernel(
    ids_smem, place_smem, ids_ref, points_ref, cent_ref, inner_ref, outer_ref, books_ref, *refs
):
    rebuilt_ref, payload_ref, hi_win, mid_win, lo_win, picks, ids_col, resid, books_low, norms, totals, mass, gaps = refs[-13:]
    base = place_smem[0]
    subs, codes, subdim = books_ref.shape
    rate = 1.0 / (math.sqrt(subdim) * math.log(2.0))
    own = cent_ref.shape[0]
    slots = own + 2 * RIM
    rows = points_ref.shape[0]
    tiles = rows // TILE
    lane = lax.broadcasted_iota(jnp.int32, (1, DEPTH), 1)
    pattern = jnp.where(lane < PIECES * SPAN, lax.rem(lane, SPAN), -1)

    def pick_rows(tile, start, low, high):
        ids = ids_col[tile * TILE : tile * TILE + TILE, :]
        ids = jnp.where((ids >= low) & (ids < high), ids - start, -2)
        parts = [(ids == pattern[:, k * 128 : k * 128 + 128]).astype(jnp.float32) for k in range(DEPTH // 128)]
        return jnp.concatenate(parts, axis=1).astype(jnp.bfloat16)

    def split(value, at):
        at = slice(at, at + value.shape[0])
        hi = value.astype(jnp.bfloat16)
        rest = value - hi.astype(jnp.float32)
        mid = rest.astype(jnp.bfloat16)
        hi_win[at] = hi
        mid_win[at] = mid
        lo_win[at] = (rest - mid.astype(jnp.float32)).astype(jnp.bfloat16)

    @pl.when(pl.program_id(0) == 0)
    def _():
        note_gaps(ids_smem, ids_ref, base, slots, gaps)
        for k in range(rows // 128):
            ids_col[k * 128 : k * 128 + 128, :] = jnp.broadcast_to(ids_ref[k : k + 1, :] - base, (128, 128)).T
        for tile in range(tiles):
            head, tail, _ = window_starts(ids_smem, base, tile, slots)
            picks[tile, :, :DEPTH] = pick_rows(tile, head, head, head + SPAN)
            picks[tile, :, DEPTH:] = pick_rows(tile, tail, jnp.maximum(tail, head + SPAN), tail + SPAN)

    first = place_smem[2] == 0
    split(jnp.where(first, outer_ref[...], inner_ref[...]), 0)
    split(cent_ref[...], RIM)
    split(jnp.where(first, inner_ref[...], outer_ref[...]), RIM + own)
    for j in range(subs):
        words = books_ref[j]
        books_low[j] = words.astype(jnp.bfloat16)
        norms[j] = jnp.broadcast_to(jnp.sum(words * words, axis=1, keepdims=True) * rate, (codes, 128))

    def window(start):
        at = pl.ds(pl.multiple_of(start, 16), SPAN)
        rest = jnp.zeros((DEPTH - PIECES * SPAN, COLS), jnp.bfloat16)
        return [hi_win[at, :], mid_win[at, :], lo_win[at, :], rest]

    def subtract(tile):
        at = slice(tile * TILE, tile * TILE + TILE)
        head, tail, _ = window_starts(ids_smem, base, tile, slots)
        both = jnp.concatenate(window(head) + window(tail), axis=0)
        got = jnp.dot(picks[tile], both, preferred_element_type=jnp.float32)
        resid[at, :] = (points_ref[at, :].astype(jnp.float32) - got).astype(jnp.bfloat16)

    for tile in range(tiles):
        subtract(tile)

    @pl.when(gaps[0] > 0)
    def _():
        for tile in range(tiles):
            at = slice(tile * TILE, tile * TILE + TILE)

            def redo(start, low, high):
                pick = pick_rows(tile, start, low, high)
                got = jnp.dot(pick, jnp.concatenate(window(start), axis=0), preferred_element_type=jnp.float32)
                fresh = points_ref[at, :].astype(jnp.float32) - got
                ids = ids_col[at, :]
                new = (ids >= low) & (ids < high)
                for k in range(COLS // 128):
                    cols = slice(k * 128, k * 128 + 128)
                    kept = resid[at, cols].astype(jnp.float32)
                    resid[at, cols] = jnp.where(new, fresh[:, cols], kept).astype(jnp.bfloat16)

            middle_windows(ids_smem, base, tile, slots, redo)

    units = [(j, c) for j in range(subs) for c in range(rows // CHUNK)]

    def place(unit):
        j, c = unit
        return slice(c * CHUNK, c * CHUNK + CHUNK), slice(j * subdim, j * subdim + subdim)

    def dots_of(unit):
        return lax.dot_general(books_low[unit[0]], resid[place(unit)], NT, preferred_element_type=jnp.float32)

    def weigh(unit, dots):
        j, c = unit
        low, over_rows = [], None
        for part in range(CHUNK // 128):
            logits = dots[:, part * 128 : part * 128 + 128] * (2.0 * rate) - norms[j]
            top = jnp.max(logits, axis=0, keepdims=True)
            raised = jnp.exp2(logits - top)
            weights = raised * (1.0 / jnp.sum(raised, axis=0, keepdims=True))
            low.append(weights.astype(jnp.bfloat16))
            over_rows = weights if over_rows is None else over_rows + weights
        mass[j] = over_rows if c == 0 else mass[j] + over_rows
        return jnp.concatenate(low, axis=1)

    def products(unit, weights_low):
        j, c = unit
        got = jnp.dot(weights_low, resid[place(unit)], preferred_element_type=jnp.float32)
        totals[j] = got if c == 0 else totals[j] + got
        rebuilt = lax.dot_general(weights_low, books_low[j], TN, preferred_element_type=jnp.float32)
        rebuilt_ref[place(unit)] = rebuilt.astype(jnp.bfloat16)

    dots, weights_low = dots_of(units[0]), None
    for n, unit in enumerate(units):
        ahead = dots_of(units[n + 1]) if n + 1 < len(units) else None
        fresh = weigh(unit, dots)
        if n > 0:
            products(units[n - 1], weights_low)
        dots, weights_low = ahead, fresh
    products(units[-1], weights_low)

    group = payload_ref.shape[1] - 8
    left = lax.broadcasted_iota(jnp.int32, (8, 128), 1) < 64
    for j in range(subs):
        for g in range(codes // group):
            at = slice(g * group, g * group + group)
            slot = j * (codes // group) + g
            payload_ref[slot, :group, :] = totals[j, at, :]
            part = mass[j, at, :]
            part = part + pltpu.roll(part, 64, 1)
            payload_ref[slot, group:, :] = jnp.where(left, part[:8], part[8:])


def reduce_kernel(prior, parts_ref, book_ref, out_ref):
    total = jnp.sum(parts_ref[...], axis=0)
    group = book_ref.shape[0]
    left = lax.broadcasted_iota(jnp.int32, (8, 128), 1) < 64
    packed = total[group:]
    mass = jnp.concatenate(
        [
            jnp.sum(jnp.where(left, packed, 0.0), axis=1, keepdims=True),
            jnp.sum(jnp.where(left, 0.0, packed), axis=1, keepdims=True),
        ],
        axis=0,
    )
    moved = (total[:group] + prior * book_ref[...]) / (mass + prior)
    out_ref[...] = jnp.broadcast_to(moved[None], out_ref.shape)


def whole(shape):
    return pl.BlockSpec(shape, lambda *_: (0,) * len(shape))


def quantize(assign, place, ids, points, centroids, inner, outer, books, owners, rebuilt):
    rows_here, width = points.shape
    half, codes, subdim = books.shape
    own = centroids.shape[0]
    subs = COLS // subdim
    steps = half // subs
    group = half * codes // owners
    slots = own + 2 * RIM

    def columns(count):
        return pl.BlockSpec((count, COLS), lambda i, ids, place: (0, place[1] + i))

    in_specs = [
        whole(ids.shape), columns(rows_here), columns(own), columns(RIM), columns(RIM),
        pl.BlockSpec((subs, codes, subdim), lambda i, *_: (i, 0, 0)),
    ]
    inputs = [assign, place, ids, points, centroids, inner, outer, books]
    aliases = {}
    if rebuilt is not None:
        aliases = {len(inputs): 0}
        in_specs.append(pl.BlockSpec(memory_space=pl.ANY))
        inputs.append(rebuilt)
    return pl.pallas_call(
        quant_kernel,
        grid_spec=pltpu.PrefetchScalarGridSpec(
            num_scalar_prefetch=2,
            grid=(steps,),
            in_specs=in_specs,
            out_specs=[columns(rows_here), pl.BlockSpec((owners // steps, group + 8, subdim), lambda i, *_: (i, 0, 0))],
            scratch_shapes=[pltpu.VMEM((slots, COLS), jnp.bfloat16)] * 3
            + [
                pltpu.VMEM((rows_here // TILE, TILE, 2 * DEPTH), jnp.bfloat16),
                pltpu.VMEM((rows_here, 128), jnp.int32),
                pltpu.VMEM((rows_here, COLS), jnp.bfloat16),
                pltpu.VMEM((subs, codes, subdim), jnp.bfloat16),
                pltpu.VMEM((subs, codes, 128), jnp.float32),
                pltpu.VMEM((subs, codes, subdim), jnp.float32),
                pltpu.VMEM((subs, codes, 128), jnp.float32),
                pltpu.SMEM((1,), jnp.int32),
            ],
        ),
        out_shape=[
            jax.ShapeDtypeStruct(points.shape, jnp.bfloat16),
            jax.ShapeDtypeStruct((owners, group + 8, subdim), jnp.float32),
        ],
        input_output_aliases=aliases,
        compiler_params=pltpu.CompilerParams(vmem_limit_bytes=58 * 1024 * 1024),
        cost_estimate=pl.CostEstimate(flops=4 * 10**9, bytes_accessed=6 * 10**6, transcendentals=2 * 10**6),
        name="quantize",
    )(*inputs)


def cluster_sums(assign, place, ids, points, counts, centroids):
    rows_here, width = points.shape
    own = centroids.shape[0]

    def columns(count):
        return pl.BlockSpec((count, COLS), lambda i, *_: (0, i))

    return pl.pallas_call(
        sums_kernel,
        grid_spec=pltpu.PrefetchScalarGridSpec(
            num_scalar_prefetch=2,
            grid=(width // COLS,),
            in_specs=[whole(ids.shape), columns(rows_here), whole(counts.shape), columns(own)],
            out_specs=[columns(own), columns(RIM), columns(RIM)],
            scratch_shapes=[
                pltpu.VMEM((own + 2 * RIM, COLS), jnp.float32),
                pltpu.VMEM((rows_here // TILE, 2 * SPAN, TILE), jnp.bfloat16),
                pltpu.SMEM((1,), jnp.int32),
            ],
        ),
        out_shape=[
            jax.ShapeDtypeStruct(centroids.shape, jnp.float32),
            jax.ShapeDtypeStruct((RIM, width), jnp.bfloat16),
            jax.ShapeDtypeStruct((RIM, width), jnp.bfloat16),
        ],
        compiler_params=pltpu.CompilerParams(vmem_limit_bytes=58 * 1024 * 1024),
        cost_estimate=pl.CostEstimate(flops=2 * 10**9, bytes_accessed=8 * 10**6, transcendentals=0),
        name="cluster_sums",
    )(assign, place, ids, points, counts, centroids)


def body(points, assign, cluster_counts, centroids, codebook):
    own, width = centroids.shape
    rows_here = points.shape[0]
    half, codes, subdim = codebook.shape
    rows_axis, sub_axis = MESH_AXES
    owners = lax.axis_size(rows_axis)
    places = owners * lax.axis_size(sub_axis)
    sub = lax.axis_index(sub_axis)
    position = lax.axis_index(rows_axis) * lax.axis_size(sub_axis) + sub
    base = position * own - RIM
    blocks = half * subdim // COLS
    swap = [(0, 1), (1, 0)]
    pairs = [(i, i + 1) for i in range(1, places - 1, 2)]
    across = pairs + [(j, i) for i, j in pairs]
    other_book = lax.ppermute(codebook, sub_axis, swap)
    outer = lax.dynamic_slice_in_dim(centroids, sub * (own - RIM), RIM, 0)
    inner = lax.dynamic_slice_in_dim(centroids, (1 - sub) * (own - RIM), RIM, 0)
    outer = lax.ppermute(outer, MESH_AXES, across)
    inner = lax.ppermute(inner, sub_axis, swap)
    ids = assign.reshape(rows_here // 128, 128)
    counts = cluster_counts.reshape(own // 128, 128)
    group = half * codes // owners

    theirs = jnp.stack([base, (1 - sub) * blocks, sub]).astype(jnp.int32)
    mine = jnp.stack([base, sub * blocks, sub]).astype(jnp.int32)
    sums, sum_inner, sum_outer = cluster_sums(assign, mine, ids, points, counts, centroids)
    theirs = lax.optimization_barrier((theirs, sum_inner))[0]
    rebuilt, away = quantize(assign, theirs, ids, points, centroids, inner, outer, other_book, owners, None)
    arrived = lax.ppermute(away, sub_axis, swap)
    rebuilt, kept = quantize(assign, mine, ids, points, centroids, inner, outer, codebook, owners, rebuilt)

    parts = lax.all_to_all(kept + arrived, rows_axis, 0, 0, tiled=True)
    book_rows = lax.dynamic_slice_in_dim(
        codebook.reshape(half * codes, subdim), lax.axis_index(rows_axis) * group, group, 0
    )
    prior = rows_here * places / codes
    moved = pl.pallas_call(
        functools.partial(reduce_kernel, prior),
        out_shape=jax.ShapeDtypeStruct((owners, group, subdim), jnp.float32),
        compiler_params=pltpu.CompilerParams(vmem_limit_bytes=8 * 1024 * 1024),
        name="moved_codes",
    )(parts, book_rows)
    moved, sum_inner, sum_outer = lax.optimization_barrier((moved, sum_inner, sum_outer))
    sum_outer = lax.ppermute(sum_outer, MESH_AXES, across)
    sum_inner = lax.ppermute(sum_inner, sub_axis, swap)
    moved = lax.all_to_all(moved, rows_axis, 0, 0, tiled=True)

    edge = pl.BlockSpec((RIM, width), lambda i, *_: (i * (own // RIM - 1), 0))
    moved_centroids = pl.pallas_call(
        edge_kernel,
        grid_spec=pltpu.PrefetchScalarGridSpec(
            num_scalar_prefetch=1,
            grid=(2,),
            in_specs=[edge, whole((RIM, width)), whole((RIM, width)), whole(counts.shape), edge],
            out_specs=edge,
        ),
        out_shape=jax.ShapeDtypeStruct(centroids.shape, jnp.float32),
        input_output_aliases={1: 0},
        compiler_params=pltpu.CompilerParams(vmem_limit_bytes=8 * 1024 * 1024),
        name="edge_clusters",
    )(mine, sums, sum_inner, sum_outer, counts, centroids)
    return (rebuilt, moved_centroids, moved.reshape(codebook.shape))


def solution(mesh):
    both = P(("rows", "sub"), None)
    flat = P(("rows", "sub"))
    books = P("sub", None, None)
    return jax.shard_map(
        body,
        mesh=mesh,
        in_specs=(both, flat, flat, both, books),
        out_specs=(both, both, books),
        check_vma=False,
    )
```

```python
import functools
import math

import jax
import jax.numpy as jnp
from jax import lax
from jax.experimental import pallas as pl
from jax.experimental.pallas import tpu as pltpu
from jax.sharding import PartitionSpec as P

RIM = 64
SPILL = 512
TILE = 256
CHUNK = 512
COLS = 256
WIDE = 512
SPAN = 80
PIECES = 3
DEPTH = 256
MESH_AXES = ("rows", "sub")
NT = (((1,), (1,)), ((), ()))
TN = (((0,), (0,)), ((), ()))


def window_starts(ids_smem, base, tile, slots):
    first = ids_smem[tile * TILE] - base
    last = ids_smem[tile * TILE + TILE - 1] - base
    head = jnp.minimum((first // 16) * 16, slots - SPAN)
    tail = jnp.clip((last // 16) * 16 - (SPAN - 16), 0, slots - SPAN)
    return pl.multiple_of(head, 16), pl.multiple_of(tail, 16), last


def note_gaps(ids_smem, ids_ref, base, first, tiles, slots, gaps):
    per = TILE // 128
    missed = jnp.zeros((per, 128), jnp.float32)
    for tile in range(tiles):
        head, tail, _ = window_starts(ids_smem, base, first + tile, slots)
        ids = ids_ref[pl.ds((first + tile) * per, per), :] - base
        missed = jnp.where((ids >= head + SPAN) & (ids < tail), 1.0, missed)
    gaps[0] = jnp.max(missed).astype(jnp.int32)


def middle_windows(ids_smem, base, tile, slots, use):
    head, tail, _ = window_starts(ids_smem, base, tile, slots)

    def step(n, carry):
        at = pl.multiple_of(head + (n + 1) * SPAN, 16)
        use(jnp.minimum(at, slots - SPAN), at, jnp.minimum(at + SPAN, tail))
        return carry

    count = (jnp.maximum(tail - head - SPAN, 0) + SPAN - 1) // SPAN
    lax.fori_loop(0, count, step, 0)


def sums_kernel(
    ids_smem, place_smem, ids_ref, points_ref, counts_ref, cent_ref, moved_ref, inner_ref, outer_ref, acc, picks, gaps
):
    base = place_smem[0]
    own = cent_ref.shape[0]
    slots = own + 2 * RIM
    per = TILE // 128
    tiles = points_ref.shape[0] // TILE

    def pick_slots(tile, start, low, high):
        ids = jnp.concatenate([ids_ref[tile * per + k : tile * per + k + 1, :] for k in range(per)], axis=1) - base
        ids = jnp.where((ids >= low) & (ids < high), ids - start, -1)
        slot = lax.broadcasted_iota(jnp.int32, (SPAN, TILE), 0)
        return (slot == ids).astype(jnp.float32).astype(jnp.bfloat16)

    @pl.when(pl.program_id(0) == 0)
    def _():
        note_gaps(ids_smem, ids_ref, base, 0, tiles, slots, gaps)
        for tile in range(tiles):
            head, tail, _ = window_starts(ids_smem, base, tile, slots)
            picks[tile, :SPAN] = pick_slots(tile, head, head, head + SPAN)
            picks[tile, SPAN:] = pick_slots(tile, tail, jnp.maximum(tail, head + SPAN), tail + SPAN)

    acc[...] = jnp.zeros_like(acc)
    sums = [
        jnp.dot(picks[tile], points_ref[tile * TILE : tile * TILE + TILE, :], preferred_element_type=jnp.float32)
        for tile in range(tiles)
    ]
    for tile in range(tiles):
        head, tail, _ = window_starts(ids_smem, base, tile, slots)
        acc[pl.ds(head, SPAN), :] += sums[tile][:SPAN]
        acc[pl.ds(tail, SPAN), :] += sums[tile][SPAN:]

    @pl.when(gaps[0] > 0)
    def _():
        for tile in range(tiles):
            rows = slice(tile * TILE, tile * TILE + TILE)

            def add(start, low, high):
                start = pl.multiple_of(start, 16)
                pick = pick_slots(tile, start, low, high)
                acc[pl.ds(start, SPAN), :] += jnp.dot(pick, points_ref[rows, :], preferred_element_type=jnp.float32)

            middle_windows(ids_smem, base, tile, slots, add)

    down = acc[:RIM].astype(jnp.bfloat16)
    up = acc[RIM + own :].astype(jnp.bfloat16)
    first = place_smem[1] == 0
    inner_ref[...] = jnp.where(first, up, down)
    outer_ref[...] = jnp.where(first, down, up)
    for part in range(own // 128):
        count = jnp.broadcast_to(counts_ref[part : part + 1, :], (128, 128)).astype(jnp.float32)
        inverse = (1.0 / (count + 2.0)).T
        lo = RIM if part == 0 else 0
        hi = 128 - RIM if part == own // 128 - 1 else 128
        at = slice(part * 128 + lo, part * 128 + hi)
        for col in range(COLS // 128):
            cols = slice(col * 128, col * 128 + 128)
            moved_ref[at, cols] = (
                acc[RIM + part * 128 + lo : RIM + part * 128 + hi, cols] + 2.0 * cent_ref[at, cols]
            ) * inverse[lo:hi]
    moved_ref[:RIM, :] = acc[RIM : 2 * RIM]
    moved_ref[own - RIM :, :] = acc[own : own + RIM]


def edge_kernel(place_smem, moved_in, inner_in, outer_in, counts_ref, cent_ref, moved_ref):
    which = pl.program_id(0)
    row = jnp.where(which == 0, 0, counts_ref.shape[0] - 1)
    count = jnp.broadcast_to(counts_ref[pl.ds(row, 1), :], (128, 128)).astype(jnp.float32)
    inverse = (1.0 / (count + 2.0)).T
    inverse = jnp.where(which == 0, inverse[:RIM], inverse[RIM:])
    outer = which == place_smem[1]
    spread = jnp.where(outer, outer_in[...].astype(jnp.float32), inner_in[...].astype(jnp.float32))
    for col in range(cent_ref.shape[1] // 128):
        cols = slice(col * 128, col * 128 + 128)
        moved_ref[:, cols] = (moved_in[:, cols] + spread[:, cols] + 2.0 * cent_ref[:, cols]) * inverse


def quant_kernel(
    first_at, extend, ids_smem, place_smem, ids_ref, points_ref, cent_ref, inner_ref, outer_ref, books_ref, *refs
):
    rebuilt_ref, payload_ref, hi_win, mid_win, lo_win, picks, ids_col, resid, books_low, norms, totals, mass, gaps = refs[-13:]
    base = place_smem[0]
    subs, codes, subdim = books_ref.shape
    rate = 1.0 / (math.sqrt(subdim) * math.log(2.0))
    own = cent_ref.shape[0]
    slots = own + 2 * RIM
    rows = points_ref.shape[0]
    tiles = rows // TILE
    first_tile = 0 if first_at is None else place_smem[first_at]
    lane = lax.broadcasted_iota(jnp.int32, (1, DEPTH), 1)
    pattern = jnp.where(lane < PIECES * SPAN, lax.rem(lane, SPAN), -1)

    def pick_rows(tile, start, low, high):
        ids = ids_col[tile * TILE : tile * TILE + TILE, :]
        ids = jnp.where((ids >= low) & (ids < high), ids - start, -2)
        parts = [(ids == pattern[:, k * 128 : k * 128 + 128]).astype(jnp.float32) for k in range(DEPTH // 128)]
        return jnp.concatenate(parts, axis=1).astype(jnp.bfloat16)

    def split(value, at):
        at = slice(at, at + value.shape[0])
        hi = value.astype(jnp.bfloat16)
        rest = value - hi.astype(jnp.float32)
        mid = rest.astype(jnp.bfloat16)
        hi_win[at] = hi
        mid_win[at] = mid
        lo_win[at] = (rest - mid.astype(jnp.float32)).astype(jnp.bfloat16)

    @pl.when(pl.program_id(0) == 0)
    def _():
        note_gaps(ids_smem, ids_ref, base, first_tile, tiles, slots, gaps)
        for k in range(rows // 128):
            ids_col[k * 128 : k * 128 + 128, :] = jnp.broadcast_to(
                ids_ref[pl.ds(first_tile * (TILE // 128) + k, 1), :] - base, (128, 128)
            ).T
        for tile in range(tiles):
            head, tail, _ = window_starts(ids_smem, base, first_tile + tile, slots)
            picks[tile, :, :DEPTH] = pick_rows(tile, head, head, head + SPAN)
            picks[tile, :, DEPTH:] = pick_rows(tile, tail, jnp.maximum(tail, head + SPAN), tail + SPAN)

    first = place_smem[1] == 0
    split(jnp.where(first, outer_ref[...], inner_ref[...]), 0)
    split(cent_ref[...], RIM)
    split(jnp.where(first, inner_ref[...], outer_ref[...]), RIM + own)
    for j in range(subs):
        words = books_ref[j]
        books_low[j] = words.astype(jnp.bfloat16)
        norms[j] = jnp.broadcast_to(jnp.sum(words * words, axis=1, keepdims=True) * rate, (codes, 128))

    def window(start):
        at = pl.ds(pl.multiple_of(start, 16), SPAN)
        rest = jnp.zeros((DEPTH - PIECES * SPAN, WIDE), jnp.bfloat16)
        return [hi_win[at, :], mid_win[at, :], lo_win[at, :], rest]

    def subtract(tile):
        at = slice(tile * TILE, tile * TILE + TILE)
        head, tail, _ = window_starts(ids_smem, base, first_tile + tile, slots)
        both = jnp.concatenate(window(head) + window(tail), axis=0)
        got = jnp.dot(picks[tile], both, preferred_element_type=jnp.float32)
        resid[at, :] = (points_ref[at, :].astype(jnp.float32) - got).astype(jnp.bfloat16)

    for tile in range(tiles):
        subtract(tile)

    @pl.when(gaps[0] > 0)
    def _():
        for tile in range(tiles):
            at = slice(tile * TILE, tile * TILE + TILE)

            def redo(start, low, high):
                pick = pick_rows(tile, start, low, high)
                got = jnp.dot(pick, jnp.concatenate(window(start), axis=0), preferred_element_type=jnp.float32)
                fresh = points_ref[at, :].astype(jnp.float32) - got
                ids = ids_col[at, :]
                new = (ids >= low) & (ids < high)
                for k in range(WIDE // 128):
                    cols = slice(k * 128, k * 128 + 128)
                    kept = resid[at, cols].astype(jnp.float32)
                    resid[at, cols] = jnp.where(new, fresh[:, cols], kept).astype(jnp.bfloat16)

            middle_windows(ids_smem, base, first_tile + tile, slots, redo)

    units = [(j, c) for j in range(subs) for c in range(rows // CHUNK)]

    def place(unit):
        j, c = unit
        return slice(c * CHUNK, c * CHUNK + CHUNK), slice(j * subdim, j * subdim + subdim)

    def dots_of(unit):
        return lax.dot_general(books_low[unit[0]], resid[place(unit)], NT, preferred_element_type=jnp.float32)

    def weigh(unit, dots):
        j, c = unit
        low, over_rows = [], None
        for part in range(CHUNK // 128):
            logits = dots[:, part * 128 : part * 128 + 128] * (2.0 * rate) - norms[j]
            top = jnp.max(logits, axis=0, keepdims=True)
            raised = jnp.exp2(logits - top)
            weights = raised * (1.0 / jnp.sum(raised, axis=0, keepdims=True))
            low.append(weights.astype(jnp.bfloat16))
            over_rows = weights if over_rows is None else over_rows + weights
        mass[j] = over_rows if c == 0 else mass[j] + over_rows
        return jnp.concatenate(low, axis=1)

    def products(unit, weights_low):
        j, c = unit
        got = jnp.dot(weights_low, resid[place(unit)], preferred_element_type=jnp.float32)
        totals[j] = got if c == 0 else totals[j] + got
        rebuilt = lax.dot_general(weights_low, books_low[j], TN, preferred_element_type=jnp.float32)
        rebuilt_ref[place(unit)] = rebuilt.astype(jnp.bfloat16)

    dots, weights_low = dots_of(units[0]), None
    for n, unit in enumerate(units):
        ahead = dots_of(units[n + 1]) if n + 1 < len(units) else None
        fresh = weigh(unit, dots)
        if n > 0:
            products(units[n - 1], weights_low)
        dots, weights_low = ahead, fresh
    products(units[-1], weights_low)

    group = payload_ref.shape[1] - 8
    left = lax.broadcasted_iota(jnp.int32, (8, 128), 1) < 64
    for j in range(subs):
        for g in range(codes // group):
            at = slice(g * group, g * group + group)
            slot = j * (codes // group) + g
            total = totals[j, at, :]
            part = mass[j, at, :]
            part = part + pltpu.roll(part, 64, 1)
            part = jnp.where(left, part[:8], part[8:])
            if extend:
                total = total + refs[0][slot, :group, :]
                part = part + refs[0][slot, group:, :]
            payload_ref[slot, :group, :] = total
            payload_ref[slot, group:, :] = part


def reduce_kernel(prior, parts_ref, book_ref, out_ref):
    total = jnp.sum(parts_ref[...], axis=0)
    group = book_ref.shape[0]
    left = lax.broadcasted_iota(jnp.int32, (8, 128), 1) < 64
    packed = total[group:]
    mass = jnp.concatenate(
        [
            jnp.sum(jnp.where(left, packed, 0.0), axis=1, keepdims=True),
            jnp.sum(jnp.where(left, 0.0, packed), axis=1, keepdims=True),
        ],
        axis=0,
    )
    moved = (total[:group] + prior * book_ref[...]) / (mass + prior)
    out_ref[...] = jnp.broadcast_to(moved[None], out_ref.shape)


def whole(shape):
    return pl.BlockSpec(shape, lambda *_: (0,) * len(shape))


def quantize(assign, place, half_at, first_at, rows, ids, points, centroids, inner, outer, books, owners, payload, rebuilt):
    width = points.shape[1]
    half, codes, subdim = books.shape
    own = centroids.shape[0]
    subs = WIDE // subdim
    steps = half // subs
    group = half * codes // owners
    slots = own + 2 * RIM

    def columns(count):
        return pl.BlockSpec((count, WIDE), lambda i, ids, place: (0, place[half_at] + i))

    if first_at is None:
        block = columns(rows)
    else:
        block = pl.BlockSpec(
            (pl.Element(rows), pl.Element(WIDE)),
            lambda i, ids, place: (
                pl.multiple_of(place[first_at] * TILE, TILE),
                pl.multiple_of((place[half_at] + i) * WIDE, WIDE),
            ),
        )
    sums = pl.BlockSpec((owners // steps, group + 8, subdim), lambda i, *_: (i, 0, 0))
    in_specs = [
        whole(ids.shape), block, columns(own), columns(RIM), columns(RIM),
        pl.BlockSpec((subs, codes, subdim), lambda i, *_: (i, 0, 0)),
    ]
    inputs = [assign, place, ids, points, centroids, inner, outer, books]
    aliases = {}
    if payload is not None:
        in_specs.append(sums)
        inputs.append(payload)
    if rebuilt is not None:
        aliases = {len(inputs): 0}
        in_specs.append(pl.BlockSpec(memory_space=pl.ANY))
        inputs.append(rebuilt)
    return pl.pallas_call(
        functools.partial(quant_kernel, first_at, payload is not None),
        grid_spec=pltpu.PrefetchScalarGridSpec(
            num_scalar_prefetch=2,
            grid=(steps,),
            in_specs=in_specs,
            out_specs=[block, sums],
            scratch_shapes=[pltpu.VMEM((slots, WIDE), jnp.bfloat16)] * 3
            + [
                pltpu.VMEM((rows // TILE, TILE, 2 * DEPTH), jnp.bfloat16),
                pltpu.VMEM((rows, 128), jnp.int32),
                pltpu.VMEM((rows, WIDE), jnp.bfloat16),
                pltpu.VMEM((subs, codes, subdim), jnp.bfloat16),
                pltpu.VMEM((subs, codes, 128), jnp.float32),
                pltpu.VMEM((subs, codes, subdim), jnp.float32),
                pltpu.VMEM((subs, codes, 128), jnp.float32),
                pltpu.SMEM((1,), jnp.int32),
            ],
        ),
        out_shape=[
            jax.ShapeDtypeStruct((points.shape[0], width), jnp.bfloat16),
            jax.ShapeDtypeStruct((owners, group + 8, subdim), jnp.float32),
        ],
        input_output_aliases=aliases,
        compiler_params=pltpu.CompilerParams(vmem_limit_bytes=58 * 1024 * 1024),
        cost_estimate=pl.CostEstimate(flops=2 * 10**6 * rows, bytes_accessed=3000 * rows, transcendentals=1000 * rows),
        name="quantize",
    )(*inputs)


def cluster_sums(assign, place, ids, points, counts, centroids):
    rows_here, width = points.shape
    own = centroids.shape[0]

    def columns(count):
        return pl.BlockSpec((count, COLS), lambda i, *_: (0, i))

    return pl.pallas_call(
        sums_kernel,
        grid_spec=pltpu.PrefetchScalarGridSpec(
            num_scalar_prefetch=2,
            grid=(width // COLS,),
            in_specs=[whole(ids.shape), columns(rows_here), whole(counts.shape), columns(own)],
            out_specs=[columns(own), columns(RIM), columns(RIM)],
            scratch_shapes=[
                pltpu.VMEM((own + 2 * RIM, COLS), jnp.float32),
                pltpu.VMEM((rows_here // TILE, 2 * SPAN, TILE), jnp.bfloat16),
                pltpu.SMEM((1,), jnp.int32),
            ],
        ),
        out_shape=[
            jax.ShapeDtypeStruct(centroids.shape, jnp.float32),
            jax.ShapeDtypeStruct((RIM, width), jnp.bfloat16),
            jax.ShapeDtypeStruct((RIM, width), jnp.bfloat16),
        ],
        compiler_params=pltpu.CompilerParams(vmem_limit_bytes=58 * 1024 * 1024),
        cost_estimate=pl.CostEstimate(flops=2 * 10**9, bytes_accessed=8 * 10**6, transcendentals=0),
        name="cluster_sums",
    )(assign, place, ids, points, counts, centroids)


def body(points, assign, cluster_counts, centroids, codebook):
    own, width = centroids.shape
    rows_here = points.shape[0]
    half, codes, subdim = codebook.shape
    rows_axis, sub_axis = MESH_AXES
    owners = lax.axis_size(rows_axis)
    places = owners * lax.axis_size(sub_axis)
    sub = lax.axis_index(sub_axis)
    position = lax.axis_index(rows_axis) * lax.axis_size(sub_axis) + sub
    base = position * own - RIM
    blocks = half * subdim // WIDE
    swap = [(0, 1), (1, 0)]
    pairs = [(i, i + 1) for i in range(1, places - 1, 2)]
    across = pairs + [(j, i) for i, j in pairs]
    other_book = lax.ppermute(codebook, sub_axis, swap)
    outer = lax.dynamic_slice_in_dim(centroids, sub * (own - RIM), RIM, 0)
    inner = lax.dynamic_slice_in_dim(centroids, (1 - sub) * (own - RIM), RIM, 0)
    outer = lax.ppermute(outer, MESH_AXES, across)
    inner = lax.ppermute(inner, sub_axis, swap)
    ids = assign.reshape(rows_here // 128, 128)
    counts = cluster_counts.reshape(own // 128, 128)
    group = half * codes // owners

    near = rows_here - SPILL
    place = jnp.stack(
        [base, sub, sub * blocks, (1 - sub) * blocks, (1 - sub) * (SPILL // TILE), sub * (near // TILE)]
    ).astype(jnp.int32)
    rebuilt, away = quantize(
        assign, place, 3, 4, near, ids, points, centroids, inner, inner, other_book, owners, None, None
    )
    rebuilt, away = quantize(
        assign, place, 3, 5, SPILL, ids, points, centroids, inner, outer, other_book, owners, away, rebuilt
    )
    arrived = lax.ppermute(away, sub_axis, swap)
    rebuilt, kept = quantize(
        assign, place, 2, None, rows_here, ids, points, centroids, inner, outer, codebook, owners, None, rebuilt
    )

    book_rows = lax.dynamic_slice_in_dim(
        codebook.reshape(half * codes, subdim), lax.axis_index(rows_axis) * group, group, 0
    )
    chip, book_rows, after = lax.optimization_barrier((kept + arrived, book_rows, place))
    parts = lax.all_to_all(chip, rows_axis, 0, 0, tiled=True)
    sums, sum_inner, sum_outer = cluster_sums(assign, after, ids, points, counts, centroids)
    parts, sums, sum_inner, sum_outer = lax.optimization_barrier((parts, sums, sum_inner, sum_outer))
    prior = rows_here * places / codes
    moved = pl.pallas_call(
        functools.partial(reduce_kernel, prior),
        out_shape=jax.ShapeDtypeStruct((owners, group, subdim), jnp.float32),
        compiler_params=pltpu.CompilerParams(vmem_limit_bytes=8 * 1024 * 1024),
        name="moved_codes",
    )(parts, book_rows)
    moved, sum_inner, sum_outer = lax.optimization_barrier((moved, sum_inner, sum_outer))
    sum_outer = lax.ppermute(sum_outer, MESH_AXES, across)
    sum_inner = lax.ppermute(sum_inner, sub_axis, swap)
    moved = lax.all_to_all(moved, rows_axis, 0, 0, tiled=True)

    edge = pl.BlockSpec((RIM, width), lambda i, *_: (i * (own // RIM - 1), 0))
    moved_centroids = pl.pallas_call(
        edge_kernel,
        grid_spec=pltpu.PrefetchScalarGridSpec(
            num_scalar_prefetch=1,
            grid=(2,),
            in_specs=[edge, whole((RIM, width)), whole((RIM, width)), whole(counts.shape), edge],
            out_specs=edge,
        ),
        out_shape=jax.ShapeDtypeStruct(centroids.shape, jnp.float32),
        input_output_aliases={1: 0},
        compiler_params=pltpu.CompilerParams(vmem_limit_bytes=8 * 1024 * 1024),
        name="edge_clusters",
    )(place, sums, sum_inner, sum_outer, counts, centroids)
    return (rebuilt, moved_centroids, moved.reshape(codebook.shape))


def solution(mesh):
    both = P(("rows", "sub"), None)
    flat = P(("rows", "sub"))
    books = P("sub", None, None)
    return jax.shard_map(
        body,
        mesh=mesh,
        in_specs=(both, flat, flat, both, books),
        out_specs=(both, both, books),
        check_vma=False,
    )
```

```python
import functools
import math

import jax
import jax.numpy as jnp
from jax import lax
from jax.experimental import pallas as pl
from jax.experimental.pallas import tpu as pltpu
from jax.sharding import PartitionSpec as P

RIM = 64
SPILL = 512
TILE = 256
CHUNK = 512
COLS = 256
WIDE = 512
SPAN = 80
PIECES = 3
DEPTH = 256
MESH_AXES = ("rows", "sub")
NT = (((1,), (1,)), ((), ()))
TN = (((0,), (0,)), ((), ()))


def window_starts(ids_smem, base, tile, slots):
    first = ids_smem[tile * TILE] - base
    last = ids_smem[tile * TILE + TILE - 1] - base
    head = jnp.minimum((first // 16) * 16, slots - SPAN)
    tail = jnp.clip((last // 16) * 16 - (SPAN - 16), 0, slots - SPAN)
    return pl.multiple_of(head, 16), pl.multiple_of(tail, 16), last


def note_gaps(ids_smem, ids_ref, base, first, tiles, slots, gaps):
    per = TILE // 128
    missed = jnp.zeros((per, 128), jnp.float32)
    for tile in range(tiles):
        head, tail, _ = window_starts(ids_smem, base, first + tile, slots)
        ids = ids_ref[pl.ds((first + tile) * per, per), :] - base
        missed = jnp.where((ids >= head + SPAN) & (ids < tail), 1.0, missed)
    gaps[0] = jnp.max(missed).astype(jnp.int32)


def middle_windows(ids_smem, base, tile, slots, use):
    head, tail, _ = window_starts(ids_smem, base, tile, slots)

    def step(n, carry):
        at = pl.multiple_of(head + (n + 1) * SPAN, 16)
        use(jnp.minimum(at, slots - SPAN), at, jnp.minimum(at + SPAN, tail))
        return carry

    count = (jnp.maximum(tail - head - SPAN, 0) + SPAN - 1) // SPAN
    lax.fori_loop(0, count, step, 0)


def sums_kernel(
    ids_smem, place_smem, ids_ref, points_ref, counts_ref, cent_ref, moved_ref, inner_ref, outer_ref, acc, picks, gaps
):
    base = place_smem[0]
    own = cent_ref.shape[0]
    slots = own + 2 * RIM
    per = TILE // 128
    tiles = points_ref.shape[0] // TILE

    def pick_slots(tile, start, low, high):
        ids = jnp.concatenate([ids_ref[tile * per + k : tile * per + k + 1, :] for k in range(per)], axis=1) - base
        ids = jnp.where((ids >= low) & (ids < high), ids - start, -1)
        slot = lax.broadcasted_iota(jnp.int32, (SPAN, TILE), 0)
        return (slot == ids).astype(jnp.float32).astype(jnp.bfloat16)

    @pl.when(pl.program_id(0) == 0)
    def _():
        note_gaps(ids_smem, ids_ref, base, 0, tiles, slots, gaps)
        for tile in range(tiles):
            head, tail, _ = window_starts(ids_smem, base, tile, slots)
            picks[tile, :SPAN] = pick_slots(tile, head, head, head + SPAN)
            picks[tile, SPAN:] = pick_slots(tile, tail, jnp.maximum(tail, head + SPAN), tail + SPAN)

    acc[...] = jnp.zeros_like(acc)
    sums = [
        jnp.dot(picks[tile], points_ref[tile * TILE : tile * TILE + TILE, :], preferred_element_type=jnp.float32)
        for tile in range(tiles)
    ]
    for tile in range(tiles):
        head, tail, _ = window_starts(ids_smem, base, tile, slots)
        acc[pl.ds(head, SPAN), :] += sums[tile][:SPAN]
        acc[pl.ds(tail, SPAN), :] += sums[tile][SPAN:]

    @pl.when(gaps[0] > 0)
    def _():
        for tile in range(tiles):
            rows = slice(tile * TILE, tile * TILE + TILE)

            def add(start, low, high):
                start = pl.multiple_of(start, 16)
                pick = pick_slots(tile, start, low, high)
                acc[pl.ds(start, SPAN), :] += jnp.dot(pick, points_ref[rows, :], preferred_element_type=jnp.float32)

            middle_windows(ids_smem, base, tile, slots, add)

    down = acc[:RIM].astype(jnp.bfloat16)
    up = acc[RIM + own :].astype(jnp.bfloat16)
    first = place_smem[1] == 0
    inner_ref[...] = jnp.where(first, up, down)
    outer_ref[...] = jnp.where(first, down, up)
    for part in range(own // 128):
        count = jnp.broadcast_to(counts_ref[part : part + 1, :], (128, 128)).astype(jnp.float32)
        inverse = (1.0 / (count + 2.0)).T
        lo = RIM if part == 0 else 0
        hi = 128 - RIM if part == own // 128 - 1 else 128
        at = slice(part * 128 + lo, part * 128 + hi)
        for col in range(COLS // 128):
            cols = slice(col * 128, col * 128 + 128)
            moved_ref[at, cols] = (
                acc[RIM + part * 128 + lo : RIM + part * 128 + hi, cols] + 2.0 * cent_ref[at, cols]
            ) * inverse[lo:hi]
    moved_ref[:RIM, :] = acc[RIM : 2 * RIM]
    moved_ref[own - RIM :, :] = acc[own : own + RIM]


def edge_kernel(place_smem, moved_in, inner_in, outer_in, counts_ref, cent_ref, moved_ref):
    which = pl.program_id(0)
    row = jnp.where(which == 0, 0, counts_ref.shape[0] - 1)
    count = jnp.broadcast_to(counts_ref[pl.ds(row, 1), :], (128, 128)).astype(jnp.float32)
    inverse = (1.0 / (count + 2.0)).T
    inverse = jnp.where(which == 0, inverse[:RIM], inverse[RIM:])
    outer = which == place_smem[1]
    spread = jnp.where(outer, outer_in[...].astype(jnp.float32), inner_in[...].astype(jnp.float32))
    for col in range(cent_ref.shape[1] // 128):
        cols = slice(col * 128, col * 128 + 128)
        moved_ref[:, cols] = (moved_in[:, cols] + spread[:, cols] + 2.0 * cent_ref[:, cols]) * inverse


def quant_kernel(
    first_at, extend, ids_smem, place_smem, ids_ref, points_ref, cent_ref, inner_ref, outer_ref, books_ref, *refs
):
    rebuilt_ref, payload_ref, hi_win, mid_win, lo_win, picks, ids_col, resid, books_low, norms, totals, mass, gaps = refs[-13:]
    base = place_smem[0]
    subs, codes, subdim = books_ref.shape
    rate = 1.0 / (math.sqrt(subdim) * math.log(2.0))
    own = cent_ref.shape[0]
    slots = own + 2 * RIM
    rows = points_ref.shape[0]
    tiles = rows // TILE
    first_tile = 0 if first_at is None else place_smem[first_at]
    lane = lax.broadcasted_iota(jnp.int32, (1, DEPTH), 1)
    pattern = jnp.where(lane < PIECES * SPAN, lax.rem(lane, SPAN), -1)

    def pick_rows(tile, start, low, high):
        ids = ids_col[tile * TILE : tile * TILE + TILE, :]
        ids = jnp.where((ids >= low) & (ids < high), ids - start, -2)
        parts = [(ids == pattern[:, k * 128 : k * 128 + 128]).astype(jnp.float32) for k in range(DEPTH // 128)]
        return jnp.concatenate(parts, axis=1).astype(jnp.bfloat16)

    def split(value, at):
        at = slice(at, at + value.shape[0])
        hi = value.astype(jnp.bfloat16)
        rest = value - hi.astype(jnp.float32)
        mid = rest.astype(jnp.bfloat16)
        hi_win[at] = hi
        mid_win[at] = mid
        lo_win[at] = (rest - mid.astype(jnp.float32)).astype(jnp.bfloat16)

    @pl.when(pl.program_id(0) == 0)
    def _():
        note_gaps(ids_smem, ids_ref, base, first_tile, tiles, slots, gaps)
        for k in range(rows // 128):
            ids_col[k * 128 : k * 128 + 128, :] = jnp.broadcast_to(
                ids_ref[pl.ds(first_tile * (TILE // 128) + k, 1), :] - base, (128, 128)
            ).T
        for tile in range(tiles):
            head, tail, _ = window_starts(ids_smem, base, first_tile + tile, slots)
            picks[tile, :, :DEPTH] = pick_rows(tile, head, head, head + SPAN)
            picks[tile, :, DEPTH:] = pick_rows(tile, tail, jnp.maximum(tail, head + SPAN), tail + SPAN)

    first = place_smem[1] == 0
    split(jnp.where(first, outer_ref[...], inner_ref[...]), 0)
    split(cent_ref[...], RIM)
    split(jnp.where(first, inner_ref[...], outer_ref[...]), RIM + own)
    for j in range(subs):
        words = books_ref[j]
        books_low[j] = words.astype(jnp.bfloat16)
        norms[j] = jnp.broadcast_to(jnp.sum(words * words, axis=1, keepdims=True) * rate, (codes, 128))

    def window(start):
        at = pl.ds(pl.multiple_of(start, 16), SPAN)
        rest = jnp.zeros((DEPTH - PIECES * SPAN, WIDE), jnp.bfloat16)
        return [hi_win[at, :], mid_win[at, :], lo_win[at, :], rest]

    def subtract(tile):
        at = slice(tile * TILE, tile * TILE + TILE)
        head, tail, _ = window_starts(ids_smem, base, first_tile + tile, slots)
        both = jnp.concatenate(window(head) + window(tail), axis=0)
        got = jnp.dot(picks[tile], both, preferred_element_type=jnp.float32)
        resid[at, :] = (points_ref[at, :].astype(jnp.float32) - got).astype(jnp.bfloat16)

    for tile in range(tiles):
        subtract(tile)

    @pl.when(gaps[0] > 0)
    def _():
        for tile in range(tiles):
            at = slice(tile * TILE, tile * TILE + TILE)

            def redo(start, low, high):
                pick = pick_rows(tile, start, low, high)
                got = jnp.dot(pick, jnp.concatenate(window(start), axis=0), preferred_element_type=jnp.float32)
                fresh = points_ref[at, :].astype(jnp.float32) - got
                ids = ids_col[at, :]
                new = (ids >= low) & (ids < high)
                for k in range(WIDE // 128):
                    cols = slice(k * 128, k * 128 + 128)
                    kept = resid[at, cols].astype(jnp.float32)
                    resid[at, cols] = jnp.where(new, fresh[:, cols], kept).astype(jnp.bfloat16)

            middle_windows(ids_smem, base, first_tile + tile, slots, redo)

    units = [(j, c) for j in range(subs) for c in range(rows // CHUNK)]

    def place(unit):
        j, c = unit
        return slice(c * CHUNK, c * CHUNK + CHUNK), slice(j * subdim, j * subdim + subdim)

    def dots_of(unit):
        return lax.dot_general(books_low[unit[0]], resid[place(unit)], NT, preferred_element_type=jnp.float32)

    def weigh(unit, dots):
        j, c = unit
        low, over_rows = [], None
        for part in range(CHUNK // 128):
            logits = dots[:, part * 128 : part * 128 + 128] * (2.0 * rate) - norms[j]
            top = jnp.max(logits, axis=0, keepdims=True)
            raised = jnp.exp2(logits - top)
            weights = raised * (1.0 / jnp.sum(raised, axis=0, keepdims=True))
            low.append(weights.astype(jnp.bfloat16))
            over_rows = weights if over_rows is None else over_rows + weights
        mass[j] = over_rows if c == 0 else mass[j] + over_rows
        return jnp.concatenate(low, axis=1)

    def products(unit, weights_low):
        j, c = unit
        got = jnp.dot(weights_low, resid[place(unit)], preferred_element_type=jnp.float32)
        totals[j] = got if c == 0 else totals[j] + got
        rebuilt = lax.dot_general(weights_low, books_low[j], TN, preferred_element_type=jnp.float32)
        rebuilt_ref[place(unit)] = rebuilt.astype(jnp.bfloat16)

    dots, weights_low = dots_of(units[0]), None
    for n, unit in enumerate(units):
        ahead = dots_of(units[n + 1]) if n + 1 < len(units) else None
        fresh = weigh(unit, dots)
        if n > 0:
            products(units[n - 1], weights_low)
        dots, weights_low = ahead, fresh
    products(units[-1], weights_low)

    group = payload_ref.shape[1] - 8
    left = lax.broadcasted_iota(jnp.int32, (8, 128), 1) < 64
    for j in range(subs):
        for g in range(codes // group):
            at = slice(g * group, g * group + group)
            slot = j * (codes // group) + g
            total = totals[j, at, :]
            part = mass[j, at, :]
            part = part + pltpu.roll(part, 64, 1)
            part = jnp.where(left, part[:8], part[8:])
            if extend:
                total = total + refs[0][slot, :group, :]
                part = part + refs[0][slot, group:, :]
            payload_ref[slot, :group, :] = total
            payload_ref[slot, group:, :] = part


def reduce_kernel(prior, parts_ref, book_ref, out_ref):
    total = jnp.sum(parts_ref[...], axis=0)
    group = book_ref.shape[0]
    left = lax.broadcasted_iota(jnp.int32, (8, 128), 1) < 64
    packed = total[group:]
    mass = jnp.concatenate(
        [
            jnp.sum(jnp.where(left, packed, 0.0), axis=1, keepdims=True),
            jnp.sum(jnp.where(left, 0.0, packed), axis=1, keepdims=True),
        ],
        axis=0,
    )
    moved = (total[:group] + prior * book_ref[...]) / (mass + prior)
    out_ref[...] = jnp.broadcast_to(moved[None], out_ref.shape)


def whole(shape):
    return pl.BlockSpec(shape, lambda *_: (0,) * len(shape))


def quantize(assign, place, half_at, first_at, rows, ids, points, centroids, inner, outer, books, owners, payload, rebuilt):
    width = points.shape[1]
    half, codes, subdim = books.shape
    own = centroids.shape[0]
    subs = WIDE // subdim
    steps = half // subs
    group = half * codes // owners
    slots = own + 2 * RIM

    def columns(count):
        return pl.BlockSpec((count, WIDE), lambda i, ids, place: (0, place[half_at] + i))

    if first_at is None:
        block = columns(rows)
    else:
        block = pl.BlockSpec(
            (pl.Element(rows), pl.Element(WIDE)),
            lambda i, ids, place: (
                pl.multiple_of(place[first_at] * TILE, TILE),
                pl.multiple_of((place[half_at] + i) * WIDE, WIDE),
            ),
        )
    sums = pl.BlockSpec((owners // steps, group + 8, subdim), lambda i, *_: (i, 0, 0))
    in_specs = [
        whole(ids.shape), block, columns(own), columns(RIM), columns(RIM),
        pl.BlockSpec((subs, codes, subdim), lambda i, *_: (i, 0, 0)),
    ]
    inputs = [assign, place, ids, points, centroids, inner, outer, books]
    aliases = {}
    if payload is not None:
        in_specs.append(sums)
        inputs.append(payload)
    if rebuilt is not None:
        aliases = {len(inputs): 0}
        in_specs.append(pl.BlockSpec(memory_space=pl.ANY))
        inputs.append(rebuilt)
    return pl.pallas_call(
        functools.partial(quant_kernel, first_at, payload is not None),
        grid_spec=pltpu.PrefetchScalarGridSpec(
            num_scalar_prefetch=2,
            grid=(steps,),
            in_specs=in_specs,
            out_specs=[block, sums],
            scratch_shapes=[pltpu.VMEM((slots, WIDE), jnp.bfloat16)] * 3
            + [
                pltpu.VMEM((rows // TILE, TILE, 2 * DEPTH), jnp.bfloat16),
                pltpu.VMEM((rows, 128), jnp.int32),
                pltpu.VMEM((rows, WIDE), jnp.bfloat16),
                pltpu.VMEM((subs, codes, subdim), jnp.bfloat16),
                pltpu.VMEM((subs, codes, 128), jnp.float32),
                pltpu.VMEM((subs, codes, subdim), jnp.float32),
                pltpu.VMEM((subs, codes, 128), jnp.float32),
                pltpu.SMEM((1,), jnp.int32),
            ],
        ),
        out_shape=[
            jax.ShapeDtypeStruct((points.shape[0], width), jnp.bfloat16),
            jax.ShapeDtypeStruct((owners, group + 8, subdim), jnp.float32),
        ],
        input_output_aliases=aliases,
        compiler_params=pltpu.CompilerParams(vmem_limit_bytes=52 * 1024 * 1024),
        cost_estimate=pl.CostEstimate(flops=2 * 10**6 * rows, bytes_accessed=3000 * rows, transcendentals=1000 * rows),
        name="quantize",
    )(*inputs)


def cluster_sums(assign, place, ids, points, counts, centroids):
    rows_here, width = points.shape
    own = centroids.shape[0]

    def columns(count):
        return pl.BlockSpec((count, COLS), lambda i, *_: (0, i))

    return pl.pallas_call(
        sums_kernel,
        grid_spec=pltpu.PrefetchScalarGridSpec(
            num_scalar_prefetch=2,
            grid=(width // COLS,),
            in_specs=[whole(ids.shape), columns(rows_here), whole(counts.shape), columns(own)],
            out_specs=[columns(own), columns(RIM), columns(RIM)],
            scratch_shapes=[
                pltpu.VMEM((own + 2 * RIM, COLS), jnp.float32),
                pltpu.VMEM((rows_here // TILE, 2 * SPAN, TILE), jnp.bfloat16),
                pltpu.SMEM((1,), jnp.int32),
            ],
        ),
        out_shape=[
            jax.ShapeDtypeStruct(centroids.shape, jnp.float32),
            jax.ShapeDtypeStruct((RIM, width), jnp.bfloat16),
            jax.ShapeDtypeStruct((RIM, width), jnp.bfloat16),
        ],
        compiler_params=pltpu.CompilerParams(vmem_limit_bytes=58 * 1024 * 1024),
        cost_estimate=pl.CostEstimate(flops=2 * 10**9, bytes_accessed=8 * 10**6, transcendentals=0),
        name="cluster_sums",
    )(assign, place, ids, points, counts, centroids)


def body(points, assign, cluster_counts, centroids, codebook):
    own, width = centroids.shape
    rows_here = points.shape[0]
    half, codes, subdim = codebook.shape
    rows_axis, sub_axis = MESH_AXES
    owners = lax.axis_size(rows_axis)
    places = owners * lax.axis_size(sub_axis)
    sub = lax.axis_index(sub_axis)
    position = lax.axis_index(rows_axis) * lax.axis_size(sub_axis) + sub
    base = position * own - RIM
    blocks = half * subdim // WIDE
    swap = [(0, 1), (1, 0)]
    pairs = [(i, i + 1) for i in range(1, places - 1, 2)]
    across = pairs + [(j, i) for i, j in pairs]
    other_book = lax.ppermute(codebook, sub_axis, swap)
    outer = lax.dynamic_slice_in_dim(centroids, sub * (own - RIM), RIM, 0)
    inner = lax.dynamic_slice_in_dim(centroids, (1 - sub) * (own - RIM), RIM, 0)
    outer = lax.ppermute(outer, MESH_AXES, across)
    inner = lax.ppermute(inner, sub_axis, swap)
    ids = assign.reshape(rows_here // 128, 128)
    counts = cluster_counts.reshape(own // 128, 128)
    group = half * codes // owners

    near = rows_here - SPILL
    place = jnp.stack(
        [base, sub, sub * blocks, (1 - sub) * blocks, (1 - sub) * (SPILL // TILE), sub * (near // TILE)]
    ).astype(jnp.int32)
    rebuilt, away = quantize(
        assign, place, 3, 4, near, ids, points, centroids, inner, inner, other_book, owners, None, None
    )
    rebuilt, away = quantize(
        assign, place, 3, 5, SPILL, ids, points, centroids, inner, outer, other_book, owners, away, rebuilt
    )
    arrived = lax.ppermute(away, sub_axis, swap)
    rebuilt, kept = quantize(
        assign, place, 2, None, rows_here, ids, points, centroids, inner, outer, codebook, owners, None, rebuilt
    )

    book_rows = lax.dynamic_slice_in_dim(
        codebook.reshape(half * codes, subdim), lax.axis_index(rows_axis) * group, group, 0
    )
    chip, book_rows, after = lax.optimization_barrier((kept + arrived, book_rows, place))
    parts = lax.all_to_all(chip, rows_axis, 0, 0, tiled=True)
    sums, sum_inner, sum_outer = cluster_sums(assign, after, ids, points, counts, centroids)
    parts, sums, sum_inner, sum_outer = lax.optimization_barrier((parts, sums, sum_inner, sum_outer))
    prior = rows_here * places / codes
    moved = pl.pallas_call(
        functools.partial(reduce_kernel, prior),
        out_shape=jax.ShapeDtypeStruct((owners, group, subdim), jnp.float32),
        compiler_params=pltpu.CompilerParams(vmem_limit_bytes=8 * 1024 * 1024),
        name="moved_codes",
    )(parts, book_rows)
    moved, sum_inner, sum_outer = lax.optimization_barrier((moved, sum_inner, sum_outer))
    sum_outer = lax.ppermute(sum_outer, MESH_AXES, across)
    sum_inner = lax.ppermute(sum_inner, sub_axis, swap)
    moved = lax.all_to_all(moved, rows_axis, 0, 0, tiled=True)

    edge = pl.BlockSpec((RIM, width), lambda i, *_: (i * (own // RIM - 1), 0))
    moved_centroids = pl.pallas_call(
        edge_kernel,
        grid_spec=pltpu.PrefetchScalarGridSpec(
            num_scalar_prefetch=1,
            grid=(2,),
            in_specs=[edge, whole((RIM, width)), whole((RIM, width)), whole(counts.shape), edge],
            out_specs=edge,
        ),
        out_shape=jax.ShapeDtypeStruct(centroids.shape, jnp.float32),
        input_output_aliases={1: 0},
        compiler_params=pltpu.CompilerParams(vmem_limit_bytes=8 * 1024 * 1024),
        name="edge_clusters",
    )(place, sums, sum_inner, sum_outer, counts, centroids)
    return (rebuilt, moved_centroids, moved.reshape(codebook.shape))


def solution(mesh):
    both = P(("rows", "sub"), None)
    flat = P(("rows", "sub"))
    books = P("sub", None, None)
    return jax.shard_map(
        body,
        mesh=mesh,
        in_specs=(both, flat, flat, both, books),
        out_specs=(both, both, books),
        check_vma=False,
    )
```

```python
import functools
import math

import jax
import jax.numpy as jnp
from jax import lax
from jax.experimental import pallas as pl
from jax.experimental.pallas import tpu as pltpu
from jax.sharding import PartitionSpec as P

RIM = 64
SPILL = 512
TILE = 256
CHUNK = 512
COLS = 256
WIDE = 512
SPAN = 80
PIECES = 3
DEPTH = 256
MESH_AXES = ("rows", "sub")
NT = (((1,), (1,)), ((), ()))
TN = (((0,), (0,)), ((), ()))


def window_starts(ids_smem, base, tile, slots):
    first = ids_smem[tile * TILE] - base
    last = ids_smem[tile * TILE + TILE - 1] - base
    head = jnp.minimum((first // 16) * 16, slots - SPAN)
    tail = jnp.clip((last // 16) * 16 - (SPAN - 16), 0, slots - SPAN)
    return pl.multiple_of(head, 16), pl.multiple_of(tail, 16), last


def note_gaps(ids_smem, ids_ref, base, first, tiles, slots, gaps):
    per = TILE // 128
    missed = jnp.zeros((per, 128), jnp.float32)
    for tile in range(tiles):
        head, tail, _ = window_starts(ids_smem, base, first + tile, slots)
        ids = ids_ref[pl.ds((first + tile) * per, per), :] - base
        missed = jnp.where((ids >= head + SPAN) & (ids < tail), 1.0, missed)
    gaps[0] = jnp.max(missed).astype(jnp.int32)


def middle_windows(ids_smem, base, tile, slots, use):
    head, tail, _ = window_starts(ids_smem, base, tile, slots)

    def step(n, carry):
        at = pl.multiple_of(head + (n + 1) * SPAN, 16)
        use(jnp.minimum(at, slots - SPAN), at, jnp.minimum(at + SPAN, tail))
        return carry

    count = (jnp.maximum(tail - head - SPAN, 0) + SPAN - 1) // SPAN
    lax.fori_loop(0, count, step, 0)


def sums_kernel(
    ids_smem, place_smem, ids_ref, points_ref, counts_ref, cent_ref, moved_ref, inner_ref, outer_ref, acc, picks, gaps
):
    base = place_smem[0]
    own = cent_ref.shape[0]
    slots = own + 2 * RIM
    per = TILE // 128
    tiles = points_ref.shape[0] // TILE

    def pick_slots(tile, start, low, high):
        ids = jnp.concatenate([ids_ref[tile * per + k : tile * per + k + 1, :] for k in range(per)], axis=1) - base
        ids = jnp.where((ids >= low) & (ids < high), ids - start, -1)
        slot = lax.broadcasted_iota(jnp.int32, (SPAN, TILE), 0)
        return (slot == ids).astype(jnp.float32).astype(jnp.bfloat16)

    @pl.when(pl.program_id(0) == 0)
    def _():
        note_gaps(ids_smem, ids_ref, base, 0, tiles, slots, gaps)
        for tile in range(tiles):
            head, tail, _ = window_starts(ids_smem, base, tile, slots)
            picks[tile, :SPAN] = pick_slots(tile, head, head, head + SPAN)
            picks[tile, SPAN:] = pick_slots(tile, tail, jnp.maximum(tail, head + SPAN), tail + SPAN)

    acc[...] = jnp.zeros_like(acc)
    sums = [
        jnp.dot(picks[tile], points_ref[tile * TILE : tile * TILE + TILE, :], preferred_element_type=jnp.float32)
        for tile in range(tiles)
    ]
    for tile in range(tiles):
        head, tail, _ = window_starts(ids_smem, base, tile, slots)
        acc[pl.ds(head, SPAN), :] += sums[tile][:SPAN]
        acc[pl.ds(tail, SPAN), :] += sums[tile][SPAN:]

    @pl.when(gaps[0] > 0)
    def _():
        for tile in range(tiles):
            rows = slice(tile * TILE, tile * TILE + TILE)

            def add(start, low, high):
                start = pl.multiple_of(start, 16)
                pick = pick_slots(tile, start, low, high)
                acc[pl.ds(start, SPAN), :] += jnp.dot(pick, points_ref[rows, :], preferred_element_type=jnp.float32)

            middle_windows(ids_smem, base, tile, slots, add)

    down = acc[:RIM].astype(jnp.bfloat16)
    up = acc[RIM + own :].astype(jnp.bfloat16)
    first = place_smem[1] == 0
    inner_ref[...] = jnp.where(first, up, down)
    outer_ref[...] = jnp.where(first, down, up)
    for part in range(own // 128):
        count = jnp.broadcast_to(counts_ref[part : part + 1, :], (128, 128)).astype(jnp.float32)
        inverse = (1.0 / (count + 2.0)).T
        lo = RIM if part == 0 else 0
        hi = 128 - RIM if part == own // 128 - 1 else 128
        at = slice(part * 128 + lo, part * 128 + hi)
        for col in range(COLS // 128):
            cols = slice(col * 128, col * 128 + 128)
            moved_ref[at, cols] = (
                acc[RIM + part * 128 + lo : RIM + part * 128 + hi, cols] + 2.0 * cent_ref[at, cols]
            ) * inverse[lo:hi]
    moved_ref[:RIM, :] = acc[RIM : 2 * RIM]
    moved_ref[own - RIM :, :] = acc[own : own + RIM]


def edge_kernel(place_smem, moved_in, inner_in, outer_in, counts_ref, cent_ref, moved_ref):
    which = pl.program_id(0)
    row = jnp.where(which == 0, 0, counts_ref.shape[0] - 1)
    count = jnp.broadcast_to(counts_ref[pl.ds(row, 1), :], (128, 128)).astype(jnp.float32)
    inverse = (1.0 / (count + 2.0)).T
    inverse = jnp.where(which == 0, inverse[:RIM], inverse[RIM:])
    outer = which == place_smem[1]
    spread = jnp.where(outer, outer_in[...].astype(jnp.float32), inner_in[...].astype(jnp.float32))
    for col in range(cent_ref.shape[1] // 128):
        cols = slice(col * 128, col * 128 + 128)
        moved_ref[:, cols] = (moved_in[:, cols] + spread[:, cols] + 2.0 * cent_ref[:, cols]) * inverse


def quant_kernel(
    first_at, extend, ids_smem, place_smem, ids_ref, points_ref, cent_ref, inner_ref, outer_ref, books_ref, *refs
):
    rebuilt_ref, payload_ref, hi_win, mid_win, lo_win, picks, ids_col, resid, books_low, norms, totals, mass, gaps = refs[-13:]
    base = place_smem[0]
    subs, codes, subdim = books_ref.shape
    rate = 1.0 / (math.sqrt(subdim) * math.log(2.0))
    own = cent_ref.shape[0]
    slots = own + 2 * RIM
    rows = points_ref.shape[0]
    tiles = rows // TILE
    first_tile = 0 if first_at is None else place_smem[first_at]
    lane = lax.broadcasted_iota(jnp.int32, (1, DEPTH), 1)
    pattern = jnp.where(lane < PIECES * SPAN, lax.rem(lane, SPAN), -1)

    def pick_rows(tile, start, low, high):
        ids = ids_col[tile * TILE : tile * TILE + TILE, :]
        ids = jnp.where((ids >= low) & (ids < high), ids - start, -2)
        parts = [(ids == pattern[:, k * 128 : k * 128 + 128]).astype(jnp.float32) for k in range(DEPTH // 128)]
        return jnp.concatenate(parts, axis=1).astype(jnp.bfloat16)

    def split(value, at):
        at = slice(at, at + value.shape[0])
        hi = value.astype(jnp.bfloat16)
        rest = value - hi.astype(jnp.float32)
        mid = rest.astype(jnp.bfloat16)
        hi_win[at] = hi
        mid_win[at] = mid
        lo_win[at] = (rest - mid.astype(jnp.float32)).astype(jnp.bfloat16)

    @pl.when(pl.program_id(0) == 0)
    def _():
        note_gaps(ids_smem, ids_ref, base, first_tile, tiles, slots, gaps)
        for k in range(rows // 128):
            ids_col[k * 128 : k * 128 + 128, :] = jnp.broadcast_to(
                ids_ref[pl.ds(first_tile * (TILE // 128) + k, 1), :] - base, (128, 128)
            ).T
        for tile in range(tiles):
            head, tail, _ = window_starts(ids_smem, base, first_tile + tile, slots)
            picks[tile, :, :DEPTH] = pick_rows(tile, head, head, head + SPAN)
            picks[tile, :, DEPTH:] = pick_rows(tile, tail, jnp.maximum(tail, head + SPAN), tail + SPAN)

    first = place_smem[1] == 0
    split(jnp.where(first, outer_ref[...], inner_ref[...]), 0)
    split(cent_ref[...], RIM)
    split(jnp.where(first, inner_ref[...], outer_ref[...]), RIM + own)
    for j in range(subs):
        words = books_ref[j]
        books_low[j] = words.astype(jnp.bfloat16)
        norms[j] = jnp.broadcast_to(jnp.sum(words * words, axis=1, keepdims=True) * rate, (codes, 128))

    def window(start):
        at = pl.ds(pl.multiple_of(start, 16), SPAN)
        rest = jnp.zeros((DEPTH - PIECES * SPAN, WIDE), jnp.bfloat16)
        return [hi_win[at, :], mid_win[at, :], lo_win[at, :], rest]

    def subtract(tile):
        at = slice(tile * TILE, tile * TILE + TILE)
        head, tail, _ = window_starts(ids_smem, base, first_tile + tile, slots)
        both = jnp.concatenate(window(head) + window(tail), axis=0)
        got = jnp.dot(picks[tile], both, preferred_element_type=jnp.float32)
        resid[at, :] = (points_ref[at, :].astype(jnp.float32) - got).astype(jnp.bfloat16)

    for tile in range(tiles):
        subtract(tile)

    @pl.when(gaps[0] > 0)
    def _():
        for tile in range(tiles):
            at = slice(tile * TILE, tile * TILE + TILE)

            def redo(start, low, high):
                pick = pick_rows(tile, start, low, high)
                got = jnp.dot(pick, jnp.concatenate(window(start), axis=0), preferred_element_type=jnp.float32)
                fresh = points_ref[at, :].astype(jnp.float32) - got
                ids = ids_col[at, :]
                new = (ids >= low) & (ids < high)
                for k in range(WIDE // 128):
                    cols = slice(k * 128, k * 128 + 128)
                    kept = resid[at, cols].astype(jnp.float32)
                    resid[at, cols] = jnp.where(new, fresh[:, cols], kept).astype(jnp.bfloat16)

            middle_windows(ids_smem, base, first_tile + tile, slots, redo)

    units = [(j, c) for j in range(subs) for c in range(rows // CHUNK)]

    def place(unit):
        j, c = unit
        return slice(c * CHUNK, c * CHUNK + CHUNK), slice(j * subdim, j * subdim + subdim)

    def dots_of(unit):
        return lax.dot_general(books_low[unit[0]], resid[place(unit)], NT, preferred_element_type=jnp.float32)

    def weigh(unit, dots):
        j, c = unit
        low, over_rows = [], None
        for part in range(CHUNK // 128):
            logits = dots[:, part * 128 : part * 128 + 128] * (2.0 * rate) - norms[j]
            top = jnp.max(logits, axis=0, keepdims=True)
            raised = jnp.exp2(logits - top)
            weights = raised * (1.0 / jnp.sum(raised, axis=0, keepdims=True))
            low.append(weights.astype(jnp.bfloat16))
            over_rows = weights if over_rows is None else over_rows + weights
        mass[j] = over_rows if c == 0 else mass[j] + over_rows
        return jnp.concatenate(low, axis=1)

    def products(unit, weights_low):
        j, c = unit
        got = jnp.dot(weights_low, resid[place(unit)], preferred_element_type=jnp.float32)
        totals[j] = got if c == 0 else totals[j] + got
        rebuilt = lax.dot_general(weights_low, books_low[j], TN, preferred_element_type=jnp.float32)
        rebuilt_ref[place(unit)] = rebuilt.astype(jnp.bfloat16)

    dots, weights_low = dots_of(units[0]), None
    for n, unit in enumerate(units):
        ahead = dots_of(units[n + 1]) if n + 1 < len(units) else None
        fresh = weigh(unit, dots)
        if n > 0:
            products(units[n - 1], weights_low)
        dots, weights_low = ahead, fresh
    products(units[-1], weights_low)

    group = payload_ref.shape[1] - 8
    left = lax.broadcasted_iota(jnp.int32, (8, 128), 1) < 64
    for j in range(subs):
        for g in range(codes // group):
            at = slice(g * group, g * group + group)
            slot = j * (codes // group) + g
            total = totals[j, at, :]
            part = mass[j, at, :]
            part = part + pltpu.roll(part, 64, 1)
            part = jnp.where(left, part[:8], part[8:])
            if extend:
                total = total + refs[0][slot, :group, :]
                part = part + refs[0][slot, group:, :]
            payload_ref[slot, :group, :] = total
            payload_ref[slot, group:, :] = part


def reduce_kernel(prior, parts_ref, book_ref, out_ref):
    total = jnp.sum(parts_ref[...], axis=0)
    group = book_ref.shape[0]
    left = lax.broadcasted_iota(jnp.int32, (8, 128), 1) < 64
    packed = total[group:]
    mass = jnp.concatenate(
        [
            jnp.sum(jnp.where(left, packed, 0.0), axis=1, keepdims=True),
            jnp.sum(jnp.where(left, 0.0, packed), axis=1, keepdims=True),
        ],
        axis=0,
    )
    moved = (total[:group] + prior * book_ref[...]) / (mass + prior)
    out_ref[...] = jnp.broadcast_to(moved[None], out_ref.shape)


def whole(shape):
    return pl.BlockSpec(shape, lambda *_: (0,) * len(shape))


def quantize(assign, place, half_at, first_at, rows, ids, points, centroids, inner, outer, books, owners, payload, rebuilt):
    width = points.shape[1]
    half, codes, subdim = books.shape
    own = centroids.shape[0]
    subs = WIDE // subdim
    steps = half // subs
    group = half * codes // owners
    slots = own + 2 * RIM

    def columns(count):
        return pl.BlockSpec((count, WIDE), lambda i, ids, place: (0, place[half_at] + i))

    if first_at is None:
        block = columns(rows)
    else:
        block = pl.BlockSpec(
            (pl.Element(rows), pl.Element(WIDE)),
            lambda i, ids, place: (
                pl.multiple_of(place[first_at] * TILE, TILE),
                pl.multiple_of((place[half_at] + i) * WIDE, WIDE),
            ),
        )
    sums = pl.BlockSpec((owners // steps, group + 8, subdim), lambda i, *_: (i, 0, 0))
    in_specs = [
        whole(ids.shape), block, columns(own), columns(RIM), columns(RIM),
        pl.BlockSpec((subs, codes, subdim), lambda i, *_: (i, 0, 0)),
    ]
    inputs = [assign, place, ids, points, centroids, inner, outer, books]
    aliases = {}
    if payload is not None:
        in_specs.append(sums)
        inputs.append(payload)
    if rebuilt is not None:
        aliases = {len(inputs): 0}
        in_specs.append(pl.BlockSpec(memory_space=pl.ANY))
        inputs.append(rebuilt)
    return pl.pallas_call(
        functools.partial(quant_kernel, first_at, payload is not None),
        grid_spec=pltpu.PrefetchScalarGridSpec(
            num_scalar_prefetch=2,
            grid=(steps,),
            in_specs=in_specs,
            out_specs=[block, sums],
            scratch_shapes=[pltpu.VMEM((slots, WIDE), jnp.bfloat16)] * 3
            + [
                pltpu.VMEM((rows // TILE, TILE, 2 * DEPTH), jnp.bfloat16),
                pltpu.VMEM((rows, 128), jnp.int32),
                pltpu.VMEM((rows, WIDE), jnp.bfloat16),
                pltpu.VMEM((subs, codes, subdim), jnp.bfloat16),
                pltpu.VMEM((subs, codes, 128), jnp.float32),
                pltpu.VMEM((subs, codes, subdim), jnp.float32),
                pltpu.VMEM((subs, codes, 128), jnp.float32),
                pltpu.SMEM((1,), jnp.int32),
            ],
        ),
        out_shape=[
            jax.ShapeDtypeStruct((points.shape[0], width), jnp.bfloat16),
            jax.ShapeDtypeStruct((owners, group + 8, subdim), jnp.float32),
        ],
        input_output_aliases=aliases,
        compiler_params=pltpu.CompilerParams(vmem_limit_bytes=51 * 1024 * 1024),
        cost_estimate=pl.CostEstimate(flops=2 * 10**6 * rows, bytes_accessed=3000 * rows, transcendentals=1000 * rows),
        name="quantize",
    )(*inputs)


def cluster_sums(assign, place, ids, points, counts, centroids):
    rows_here, width = points.shape
    own = centroids.shape[0]

    def columns(count):
        return pl.BlockSpec((count, COLS), lambda i, *_: (0, i))

    return pl.pallas_call(
        sums_kernel,
        grid_spec=pltpu.PrefetchScalarGridSpec(
            num_scalar_prefetch=2,
            grid=(width // COLS,),
            in_specs=[whole(ids.shape), columns(rows_here), whole(counts.shape), columns(own)],
            out_specs=[columns(own), columns(RIM), columns(RIM)],
            scratch_shapes=[
                pltpu.VMEM((own + 2 * RIM, COLS), jnp.float32),
                pltpu.VMEM((rows_here // TILE, 2 * SPAN, TILE), jnp.bfloat16),
                pltpu.SMEM((1,), jnp.int32),
            ],
        ),
        out_shape=[
            jax.ShapeDtypeStruct(centroids.shape, jnp.float32),
            jax.ShapeDtypeStruct((RIM, width), jnp.bfloat16),
            jax.ShapeDtypeStruct((RIM, width), jnp.bfloat16),
        ],
        compiler_params=pltpu.CompilerParams(vmem_limit_bytes=58 * 1024 * 1024),
        cost_estimate=pl.CostEstimate(flops=2 * 10**9, bytes_accessed=8 * 10**6, transcendentals=0),
        name="cluster_sums",
    )(assign, place, ids, points, counts, centroids)


def body(points, assign, cluster_counts, centroids, codebook):
    own, width = centroids.shape
    rows_here = points.shape[0]
    half, codes, subdim = codebook.shape
    rows_axis, sub_axis = MESH_AXES
    owners = lax.axis_size(rows_axis)
    places = owners * lax.axis_size(sub_axis)
    sub = lax.axis_index(sub_axis)
    position = lax.axis_index(rows_axis) * lax.axis_size(sub_axis) + sub
    base = position * own - RIM
    blocks = half * subdim // WIDE
    swap = [(0, 1), (1, 0)]
    pairs = [(i, i + 1) for i in range(1, places - 1, 2)]
    across = pairs + [(j, i) for i, j in pairs]
    other_book = lax.ppermute(codebook, sub_axis, swap)
    outer = lax.dynamic_slice_in_dim(centroids, sub * (own - RIM), RIM, 0)
    inner = lax.dynamic_slice_in_dim(centroids, (1 - sub) * (own - RIM), RIM, 0)
    outer = lax.ppermute(outer, MESH_AXES, across)
    inner = lax.ppermute(inner, sub_axis, swap)
    ids = assign.reshape(rows_here // 128, 128)
    counts = cluster_counts.reshape(own // 128, 128)
    group = half * codes // owners

    near = rows_here - SPILL
    place = jnp.stack(
        [base, sub, sub * blocks, (1 - sub) * blocks, (1 - sub) * (SPILL // TILE), sub * (near // TILE)]
    ).astype(jnp.int32)
    rebuilt, away = quantize(
        assign, place, 3, 4, near, ids, points, centroids, inner, inner, other_book, owners, None, None
    )
    rebuilt, away = quantize(
        assign, place, 3, 5, SPILL, ids, points, centroids, inner, outer, other_book, owners, away, rebuilt
    )
    arrived = lax.ppermute(away, sub_axis, swap)
    rebuilt, kept = quantize(
        assign, place, 2, None, rows_here, ids, points, centroids, inner, outer, codebook, owners, None, rebuilt
    )

    book_rows = lax.dynamic_slice_in_dim(
        codebook.reshape(half * codes, subdim), lax.axis_index(rows_axis) * group, group, 0
    )
    chip, book_rows, after = lax.optimization_barrier((kept + arrived, book_rows, place))
    parts = lax.all_to_all(chip, rows_axis, 0, 0, tiled=True)
    sums, sum_inner, sum_outer = cluster_sums(assign, after, ids, points, counts, centroids)
    parts, sums, sum_inner, sum_outer = lax.optimization_barrier((parts, sums, sum_inner, sum_outer))
    prior = rows_here * places / codes
    moved = pl.pallas_call(
        functools.partial(reduce_kernel, prior),
        out_shape=jax.ShapeDtypeStruct((owners, group, subdim), jnp.float32),
        compiler_params=pltpu.CompilerParams(vmem_limit_bytes=8 * 1024 * 1024),
        name="moved_codes",
    )(parts, book_rows)
    moved, sum_inner, sum_outer = lax.optimization_barrier((moved, sum_inner, sum_outer))
    sum_outer = lax.ppermute(sum_outer, MESH_AXES, across)
    sum_inner = lax.ppermute(sum_inner, sub_axis, swap)
    moved = lax.all_to_all(moved, rows_axis, 0, 0, tiled=True)

    edge = pl.BlockSpec((RIM, width), lambda i, *_: (i * (own // RIM - 1), 0))
    moved_centroids = pl.pallas_call(
        edge_kernel,
        grid_spec=pltpu.PrefetchScalarGridSpec(
            num_scalar_prefetch=1,
            grid=(2,),
            in_specs=[edge, whole((RIM, width)), whole((RIM, width)), whole(counts.shape), edge],
            out_specs=edge,
        ),
        out_shape=jax.ShapeDtypeStruct(centroids.shape, jnp.float32),
        input_output_aliases={1: 0},
        compiler_params=pltpu.CompilerParams(vmem_limit_bytes=8 * 1024 * 1024),
        name="edge_clusters",
    )(place, sums, sum_inner, sum_outer, counts, centroids)
    return (rebuilt, moved_centroids, moved.reshape(codebook.shape))


def solution(mesh):
    both = P(("rows", "sub"), None)
    flat = P(("rows", "sub"))
    books = P("sub", None, None)
    return jax.shard_map(
        body,
        mesh=mesh,
        in_specs=(both, flat, flat, both, books),
        out_specs=(both, both, books),
        check_vma=False,
    )
```
